512 devices in a mesh: rep: 64 (over x, y, core), tp: 8 (over z).
Axes of the slice: x: 4, y: 8, z: 8, core: 2. Of those that a mesh axis runs over, the one named last changes fastest.
Arguments:
- queries: bfloat16 [16384, 4096], P('rep', 'tp'), may hold values from -8 to 8
- suffix_key_rows: bfloat16 [16384, 1024], P('rep', 'tp'), may hold values from -8 to 8
- suffix_value_rows: bfloat16 [16384, 1024], P('rep', 'tp'), may hold values from -6 to 6
- mamba_input: bfloat16 [16384, 8192], P('rep', 'tp'), may hold values from -6 to 6
- mamba_gate: bfloat16 [16384, 8192], P('rep', 'tp'), may hold values from -18 to 18
- input_projection: bfloat16 [16384, 256], P('rep'), may hold values from -6 to 6
- output_projection: bfloat16 [16384, 256], P('rep'), may hold values from -6 to 6
- step_lengths: float32 [16384, 128], P('rep', 'tp'), may hold values from 0.0002 to 1
- decay_log: float32 [128], P('tp'), may hold values from -0.7 to 2.8
- skip_gain: float32 [128], P('tp'), may hold values from 0.5 to 1.5
- gated_norm_gain: float32 [8192], P('tp'), may hold values from 0.5 to 1.5
- cache_store: bfloat16 [1024, 8, 2, 128, 128], P('rep', 'tp'), may hold values from -6 to 6
- request_units: int32 [128, 56], replicated, may hold values from 0 to 1023, as said below
- prefix_block_count: int32 [128], replicated, may hold values from 8 to 48
Outputs:
- attn_out: bfloat16 [16384, 4096], P('rep', 'tp')
- mamba_out: bfloat16 [16384, 8192], P('rep', 'tp')
- final_state: bfloat16 [128, 128, 64, 256], P('rep', 'tp')
The draws below stay inside these ranges and needn't reach their ends.
Inputs may be any that keep to these rules, and one draw needn't show every extreme that they name: `request_units`: entries 0 to 47 of row q name request q's prefix blocks in order, of which the first prefix_block_count[q] are read; entries 48 onward name the units of its SSM state, all read. Unit u belongs to owner u // 16. Over the read entries of the requests 2 r to 2 r + 1 of one replica r, no owner is named more than 2 times, and in every draw some owner is named exactly 2 times by some replica.
All inputs are finite; a program needn't handle non-finite values.
Results may differ from the reference program's by a relative error of at most 0.0075.
Values may be sent and summed in bfloat16 or wider, within the bound.
A program may use at most 64 MiB of HBM per device.

```python
import math
import jax
import jax.numpy as jnp
from jax import lax

QUERY_HEADS = 32
KEY_VALUE_HEADS = 8
HEAD_WIDTH = 128
MAMBA_HEADS = 128
MAMBA_HEAD_WIDTH = 64
STATE_WIDTH = 256
BLOCK_TOKENS = 128
MAX_PREFIX_BLOCK = 48
MINB = 8
REQ_DEV = 2
SUFFIX_TOKENS = 128
UNITS_DEV = 16
STATE_UNITS = 8
REPLICAS = 64
REQUEST_TOTAL = 128
TOKEN_TOTAL = 16384
UNITS = 1024


def draw_queries(key, part):
    key = jax.random.fold_in(key, 21)
    value_matrix = jnp.clip(jax.random.normal(key, (TOKEN_TOTAL, QUERY_HEADS * HEAD_WIDTH), jnp.float32), -6.0, 6.0)
    return value_matrix.astype(jnp.bfloat16)


def draw_suffix_key_rows(key, part):
    key = jax.random.fold_in(key, 22)
    value_matrix = jnp.clip(jax.random.normal(key, (TOKEN_TOTAL, KEY_VALUE_HEADS * HEAD_WIDTH), jnp.float32), -6.0, 6.0)
    return value_matrix.astype(jnp.bfloat16)


def head_rates(key, slow_share):
    chooser = jax.random.uniform(jax.random.fold_in(key, 7), (MAMBA_HEADS,))
    levels = jax.random.uniform(jax.random.fold_in(key, 8), (MAMBA_HEADS,))
    slow_heads = chooser < slow_share
    state_magnitude = jnp.where(slow_heads, jnp.exp(math.log(0.5) + levels * math.log(4.0)), jnp.exp(math.log(4.0) + levels * math.log(4.0)))
    return (state_magnitude, slow_heads)


def draw_decay_log(key, part):
    state_magnitude, slow_heads = head_rates(key, 0.5)
    return jnp.log(state_magnitude)


def draw_step_lengths(key, part):
    state_magnitude, slow_heads = head_rates(key, 0.5)
    key = jax.random.fold_in(key, 41)
    roughness = jnp.exp(jax.random.uniform(jax.random.fold_in(key, 1), (TOKEN_TOTAL, MAMBA_HEADS), jnp.float32, -math.log(2.0), math.log(2.0)))
    steady_decay = jnp.where(slow_heads[None, :], 0.6 / (SUFFIX_TOKENS * state_magnitude[None, :]), 0.025 / state_magnitude[None, :]) * roughness
    token_groups = jax.random.bernoulli(jax.random.fold_in(key, 2), 2.0 / SUFFIX_TOKENS, (TOKEN_TOTAL, 1))
    return steady_decay + jnp.where(token_groups, 0.4 / state_magnitude[None, :], 0.0)


def draw_mamba_gate(key, part):
    key = jax.random.fold_in(key, 51)
    decay_ramp = jnp.arange(MAMBA_HEADS * MAMBA_HEAD_WIDTH, dtype=jnp.float32) / (MAMBA_HEADS * MAMBA_HEAD_WIDTH)
    value_matrix = jnp.clip(jax.random.normal(key, (TOKEN_TOTAL, MAMBA_HEADS * MAMBA_HEAD_WIDTH), jnp.float32), -6.0, 6.0) * jnp.power(3.0, decay_ramp)[None, :]
    return value_matrix.astype(jnp.bfloat16)


def draw_request_units(key, part):
    key = jax.random.fold_in(key, 11)
    positions = REQ_DEV * (MAX_PREFIX_BLOCK + STATE_UNITS)
    replica_keys = jax.random.split(jax.random.fold_in(key, 1), REPLICAS)
    orders = jax.vmap(lambda single: jax.random.permutation(single, REPLICAS))(replica_keys).astype(jnp.int32)
    ordinal = jnp.arange(positions, dtype=jnp.int32)
    owners = orders[:, ordinal % REPLICAS]
    slots = jax.random.randint(jax.random.fold_in(key, 2), (REPLICAS, positions), 0, UNITS_DEV, dtype=jnp.int32)
    return (owners * UNITS_DEV + slots).reshape(REQUEST_TOTAL, MAX_PREFIX_BLOCK + STATE_UNITS)


def draw_prefix_block_count(key, part):
    key = jax.random.fold_in(key, 61)
    blocks = jax.random.randint(key, (REQUEST_TOTAL,), MINB, MAX_PREFIX_BLOCK + 1, dtype=jnp.int32)
    return blocks.at[0].set(MAX_PREFIX_BLOCK).at[1].set(MAX_PREFIX_BLOCK).at[2].set(MINB)


def steps_of(stream_key, dims, pieces, low, top_value):
    def one(dim, parts):
        draws = jax.random.uniform(jax.random.fold_in(jax.random.fold_in(stream_key, 6), dim), (parts,), jnp.float32, low / len(pieces), top_value / len(pieces))
        return jnp.repeat(jnp.exp(draws), dims[dim] // parts).reshape((-1,) + (1,) * (len(dims) - dim - 1))

    level = one(*pieces[0])
    for cut in pieces[1:]:
        level = level * one(*cut)
    return level


def centred(own_key, dims, deviation, bound, cuts=(), held_as=jnp.bfloat16):
    loudness = steps_of(own_key, dims, cuts, -0.22, 0.18) if cuts else 1.0
    array = jax.random.normal(own_key, dims, jnp.float32) * deviation * loudness
    return jnp.minimum(jnp.maximum(array, -bound), bound).astype(held_as)


def setup_inputs(seed: int = 0) -> dict:
    streams_of = jax.random.split(jax.random.key(seed), 15)
    queries = draw_queries(jax.random.fold_in(streams_of[14], 71), 0)
    suffix_key_rows = draw_suffix_key_rows(jax.random.fold_in(streams_of[14], 71), 0)
    suffix_value_rows = centred(streams_of[2], (TOKEN_TOTAL, KEY_VALUE_HEADS * HEAD_WIDTH), 1.0, 6.0, ((0, 64), (1, 8)))
    mamba_input = centred(streams_of[3], (TOKEN_TOTAL, MAMBA_HEADS * MAMBA_HEAD_WIDTH), 1.0, 6.0, ((0, 64), (1, 8)))
    mamba_gate = draw_mamba_gate(jax.random.fold_in(streams_of[14], 71), 0)
    input_projection = centred(streams_of[5], (TOKEN_TOTAL, STATE_WIDTH), 1.0, 6.0, ((0, 64),))
    output_projection = centred(streams_of[6], (TOKEN_TOTAL, STATE_WIDTH), 1.0, 6.0, ((0, 64),))
    step_lengths = draw_step_lengths(jax.random.fold_in(streams_of[14], 71), 0)
    decay_log = draw_decay_log(jax.random.fold_in(streams_of[14], 71), 0)
    skip_gain = jnp.clip(0.5 + 1.0 * jax.random.uniform(streams_of[9], (MAMBA_HEADS,), jnp.float32) ** steps_of(streams_of[9], (MAMBA_HEADS,), ((0, 8),), -0.2, 0.2), 0.5, 1.5)
    gated_norm_gain = jnp.clip(1.0 + 0.1 * jax.random.normal(streams_of[10], (MAMBA_HEADS * MAMBA_HEAD_WIDTH,), jnp.float32), 0.5, 1.5)
    cache_store = centred(streams_of[11], (UNITS, KEY_VALUE_HEADS, 2, BLOCK_TOKENS, HEAD_WIDTH), 1.0, 6.0, ((0, 64), (1, 8)))
    request_units = draw_request_units(jax.random.fold_in(streams_of[14], 71), 0)
    prefix_block_count = draw_prefix_block_count(jax.random.fold_in(streams_of[14], 71), 0)
    return dict(queries=queries, suffix_key_rows=suffix_key_rows, suffix_value_rows=suffix_value_rows, mamba_input=mamba_input, mamba_gate=mamba_gate, input_projection=input_projection, output_projection=output_projection, step_lengths=step_lengths, decay_log=decay_log, skip_gain=skip_gain, gated_norm_gain=gated_norm_gain, cache_store=cache_store, request_units=request_units, prefix_block_count=prefix_block_count)


def reference(queries, suffix_key_rows, suffix_value_rows, mamba_input, mamba_gate, input_projection, output_projection, step_lengths, decay_log, skip_gain, gated_norm_gain, cache_store, request_units, prefix_block_count):
    highest = lax.Precision.HIGHEST
    group_size = QUERY_HEADS // KEY_VALUE_HEADS
    prefix_len = MAX_PREFIX_BLOCK * BLOCK_TOKENS
    key_index = jnp.arange(prefix_len + SUFFIX_TOKENS, dtype=jnp.int32)
    token_index = jnp.arange(SUFFIX_TOKENS, dtype=jnp.int32)
    decay_rates = -jnp.exp(decay_log)

    def serve(packed_inputs):
        query_rows, key_rows, value_rows, input_arrays, gate_matrix, b_rows, c_rows, deltas, unit_list, blocks_used = packed_inputs
        unit_contents = cache_store[unit_list].astype(jnp.float32)
        prefix = unit_contents[:MAX_PREFIX_BLOCK]
        prefix_keys = prefix[:, :, 0].transpose(1, 0, 2, 3).reshape(KEY_VALUE_HEADS, prefix_len, HEAD_WIDTH)
        prefix_values = prefix[:, :, 1].transpose(1, 0, 2, 3).reshape(KEY_VALUE_HEADS, prefix_len, HEAD_WIDTH)
        suffix_keys = key_rows.astype(jnp.float32).reshape(SUFFIX_TOKENS, KEY_VALUE_HEADS, HEAD_WIDTH).transpose(1, 0, 2)
        suffix_values = value_rows.astype(jnp.float32).reshape(SUFFIX_TOKENS, KEY_VALUE_HEADS, HEAD_WIDTH).transpose(1, 0, 2)
        all_keys = jnp.concatenate([prefix_keys, suffix_keys], axis=1)
        all_values = jnp.concatenate([prefix_values, suffix_values], axis=1)
        query_heads = query_rows.astype(jnp.float32).reshape(SUFFIX_TOKENS, KEY_VALUE_HEADS, group_size, HEAD_WIDTH).transpose(1, 2, 0, 3)
        logits = jnp.einsum('kgtd,ksd->kgts', query_heads, all_keys) / math.sqrt(HEAD_WIDTH)
        allowed = jnp.where(key_index[None, :] < prefix_len, key_index[None, :] < blocks_used * BLOCK_TOKENS, key_index[None, :] - prefix_len <= token_index[:, None])
        logits = jnp.where(allowed[None, None], logits, -1e+30)
        row_top = lax.optimization_barrier(jnp.max(logits, axis=-1, keepdims=True))
        weights = jnp.exp(logits - row_top)
        totals = lax.optimization_barrier(jnp.sum(weights, axis=-1, keepdims=True))
        rounded = lax.optimization_barrier(weights.astype(jnp.bfloat16)).astype(jnp.float32)
        blended = jnp.einsum('kgts,ksd->kgtd', rounded, all_values) / totals
        attention_layer = blended.transpose(2, 0, 1, 3).reshape(SUFFIX_TOKENS, QUERY_HEADS * HEAD_WIDTH).astype(jnp.bfloat16)
        opening_state = unit_contents[MAX_PREFIX_BLOCK:].reshape(STATE_UNITS, KEY_VALUE_HEADS, 2 * BLOCK_TOKENS * HEAD_WIDTH).transpose(1, 0, 2).reshape(MAMBA_HEADS, MAMBA_HEAD_WIDTH, STATE_WIDTH)
        running = jnp.cumsum(deltas * decay_rates[None, :], axis=0)
        input_head_rows = input_arrays.astype(jnp.float32).reshape(SUFFIX_TOKENS, MAMBA_HEADS, MAMBA_HEAD_WIDTH)
        b_float = b_rows.astype(jnp.float32)
        c_float = c_rows.astype(jnp.float32)
        products = jnp.dot(c_float, b_float.T, precision=highest)
        causal = token_index[:, None] >= token_index[None, :]
        log_gaps = jnp.where(causal[None], running.T[:, :, None] - running.T[:, None, :], -1e+30)
        kernel = jnp.exp(log_gaps) * products[None] * deltas.T[:, None, :]
        local_part = jnp.einsum('hts,shp->thp', kernel, input_head_rows, precision=highest)
        carried = jnp.exp(running)[:, :, None] * jnp.einsum('tn,hpn->thp', c_float, opening_state, precision=highest)
        output_arrays = local_part + carried + skip_gain[None, :, None] * input_head_rows
        tail_weight = jnp.exp(running[-1][None, :] - running) * deltas
        closing_state = jnp.exp(running[-1])[:, None, None] * opening_state + jnp.einsum('shp,sn->hpn', tail_weight[:, :, None] * input_head_rows, b_float, precision=highest)
        gated_output = output_arrays.reshape(SUFFIX_TOKENS, MAMBA_HEADS * MAMBA_HEAD_WIDTH) * jax.nn.silu(gate_matrix.astype(jnp.float32))
        mean_square = lax.optimization_barrier(jnp.mean(gated_output * gated_output, axis=-1, keepdims=True))
        normed_output = (gated_output * lax.rsqrt(mean_square + 1e-05) * gated_norm_gain[None, :]).astype(jnp.bfloat16)
        return (attention_layer, normed_output, closing_state.astype(jnp.bfloat16))
    packed_inputs = (queries.reshape(REQUEST_TOTAL, SUFFIX_TOKENS, QUERY_HEADS * HEAD_WIDTH), suffix_key_rows.reshape(REQUEST_TOTAL, SUFFIX_TOKENS, KEY_VALUE_HEADS * HEAD_WIDTH), suffix_value_rows.reshape(REQUEST_TOTAL, SUFFIX_TOKENS, KEY_VALUE_HEADS * HEAD_WIDTH), mamba_input.reshape(REQUEST_TOTAL, SUFFIX_TOKENS, MAMBA_HEADS * MAMBA_HEAD_WIDTH), mamba_gate.reshape(REQUEST_TOTAL, SUFFIX_TOKENS, MAMBA_HEADS * MAMBA_HEAD_WIDTH), input_projection.reshape(REQUEST_TOTAL, SUFFIX_TOKENS, STATE_WIDTH), output_projection.reshape(REQUEST_TOTAL, SUFFIX_TOKENS, STATE_WIDTH), step_lengths.reshape(REQUEST_TOTAL, SUFFIX_TOKENS, MAMBA_HEADS), request_units, prefix_block_count)
    attention_layer, normed_output, closing_state = lax.map(serve, packed_inputs)
    return (attention_layer.reshape(TOKEN_TOTAL, QUERY_HEADS * HEAD_WIDTH), normed_output.reshape(TOKEN_TOTAL, MAMBA_HEADS * MAMBA_HEAD_WIDTH), closing_state)
```

```python
import math

import jax
import jax.numpy as jnp
from jax import lax
from jax.experimental import pallas as pl
from jax.experimental.pallas import tpu as pltpu
from jax.sharding import PartitionSpec as P

MESH = pl.DeviceIdType.MESH
HEAD_WIDTH = 128
MAMBA_COLUMNS = 8192
MAX_PREFIX_BLOCK = 48
PER_REQUEST = 56
POSITIONS = 112
TOKENS = 128
XN, YN, CN, ZN = 4, 8, 2, 8
UNITS = 16
GROUP = 8
GROUPS = MAX_PREFIX_BLOCK // GROUP
ROWS = 512
PAIRS = 8
NEG = -1e30
HIGHEST = lax.Precision.HIGHEST
SCALING = 1.0 / math.sqrt(HEAD_WIDTH)
PARTNERS = [(dx, dc) for dx in range(XN) for dc in range(CN)]


def dot_nt(a, b, precision=None):
    return lax.dot_general(
        a, b, (((1,), (1,)), ((), ())), precision=precision, preferred_element_type=jnp.float32
    )


def dot_tn(a, b, precision=None):
    return lax.dot_general(
        a, b, (((0,), (0,)), ((), ())), precision=precision, preferred_element_type=jnp.float32
    )


def dot_nn(a, b, precision=None):
    return jnp.dot(a, b, precision=precision, preferred_element_type=jnp.float32)


def kernel(
    send_index, position_index, counts,
    queries, suffix_keys, suffix_values, mamba_x, mamba_gate, b_rows, c_rows,
    steps, decay_log, skip_lanes, norm_gain, cache,
    attn_out, mamba_out, final_state,
    yk, yv, pick, xk, xv, kin, vin, probs, suffix_probs, scores, query_scr,
    top, total, group_top, out_acc, products, run_col, run_row, step_row, local_y,
    closing, square_out, square_in,
    y_send, y_recv, x_send, x_recv, z_send, z_recv,
):
    rep = lax.axis_index("rep")
    tp = lax.axis_index("tp")
    x, y, c = rep // 16, (rep // 2) % YN, rep % 2

    def device(dx, dy, dc):
        return (((x + dx) % XN * YN + (y + dy) % YN) * CN + (c + dc) % CN, tp)

    barrier = pltpu.get_barrier_semaphore()
    for dx, dc in PARTNERS[1:]:
        pl.semaphore_signal(barrier, 1, device_id=device(dx, 0, dc), device_id_type=MESH)
    for dy in (1, YN - 1):
        pl.semaphore_signal(barrier, 1, device_id=device(0, dy, 0), device_id_type=MESH)
    for dz in range(1, ZN):
        pl.semaphore_signal(barrier, 1, device_id=(rep, (tp + dz) % ZN), device_id_type=MESH)
    pl.semaphore_wait(barrier, len(PARTNERS) - 1 + 2 + ZN - 1)

    ybufs, xbufs, inbufs = (yk, yv), (xk, xv), (kin, vin)

    def y_copy(phase, direction, src, ss):
        distance, half = ss // 2 + 1, ss % 2
        row = distance - 1 if direction == 0 else YN - 1 - distance
        half = half if direction == 0 else 1 - half
        dst = ybufs[phase].at[row, pl.ds(half * 8, 8)]
        slot = (direction * 2 + phase) * 7 + ss
        return pltpu.make_async_remote_copy(
            src_ref=dst if src is None else src,
            dst_ref=dst,
            send_sem=y_send.at[slot],
            recv_sem=y_recv.at[slot],
            device_id=device(0, 1 if direction == 0 else YN - 1, 0),
            device_id_type=MESH,
        )

    def y_own(phase, direction, ss):
        half = ss if direction == 0 else 1 - ss
        return y_copy(phase, direction, cache.at[pl.ds(half * 8, 8), phase], ss)

    def y_forward(phase, direction, ss):
        distance, half = ss // 2 + 1, ss % 2
        row = distance - 1 if direction == 0 else YN - 1 - distance
        half = half if direction == 0 else 1 - half
        return y_copy(phase, direction, ybufs[phase].at[row, pl.ds(half * 8, 8)], ss + 2)

    def x_copy(phase, dy, j):
        dx, dc = PARTNERS[j]
        slot = (phase * YN + dy) * 7 + j - 1
        return pltpu.make_async_remote_copy(
            src_ref=xbufs[phase].at[dy, j - 1],
            dst_ref=inbufs[phase].at[pl.ds((j * YN + dy) * 2, 2)],
            send_sem=x_send.at[slot],
            recv_sem=x_recv.at[slot],
            device_id=device(dx, 0, dc),
            device_id_type=MESH,
        )

    def send_chosen(phase, dy):
        for j, (dx, dc) in enumerate(PARTNERS):
            target = ((x + dx) % XN) * CN + (c + dc) % CN
            for s in range(2):
                unit = send_index[(dy * 8 + target) * 2 + s]
                if j == 0:
                    inbufs[phase][dy * 2 + s] = pick[unit]
                else:
                    xbufs[phase][dy, j - 1, s] = pick[unit]
            if j > 0:
                x_copy(phase, dy, j).start()

    for direction in (0, 1):
        for ss in (0, 1):
            y_own(0, direction, ss).start()
    for phase in (0, 1):
        pick[...] = cache[:, phase]
        send_chosen(phase, 0)

    lane = lax.broadcasted_iota(jnp.int32, (TOKENS, 128), 1)
    row = lax.broadcasted_iota(jnp.int32, (TOKENS, 128), 0)
    low_half = lane < 64
    lane16 = lax.broadcasted_iota(jnp.int32, (TOKENS, 16), 1)
    causal = row >= lane
    rates = -jnp.exp(decay_log[...])

    def prepare(q, carry):
        rows = pl.ds(pl.multiple_of(q * TOKENS, TOKENS), TOKENS)
        for h in range(4):
            query_scr[q, pl.ds(h * TOKENS, TOKENS)] = queries[rows, pl.ds(h * 128, 128)]
        delta = steps[rows, :]
        lower = (row >= lane).astype(jnp.float32)
        upper = (row <= lane).astype(jnp.float32)
        unit = (row == lane).astype(jnp.float32)
        run_col[q] = dot_nn(lower, delta * rates, HIGHEST)
        run_row[q] = dot_tn(delta * rates, upper, HIGHEST)
        step_row[q] = dot_tn(delta, unit, HIGHEST)
        products[q] = jnp.where(causal, dot_nt(c_rows[rows, :], b_rows[rows, :]), 0.0)
        keys = suffix_keys[rows, :]
        for h in range(4):
            part = pl.ds(h * TOKENS, TOKENS)
            s = dot_nt(query_scr[q, part], keys) * SCALING
            s = jnp.where(causal, s, NEG)
            m = jnp.broadcast_to(jnp.max(s, axis=1, keepdims=True), (TOKENS, 128))
            p = jnp.exp(s - m)
            top[q, part] = m
            group_top[q * (GROUPS + 1) + GROUPS, part] = m
            total[q, part] = p
            suffix_probs[q, part] = p.astype(jnp.bfloat16)
        return carry

    lax.fori_loop(0, 2, prepare, 0)

    def column(ref, q_rows, h):
        return jnp.sum(jnp.where(lane16 == h, ref[q_rows], 0.0), axis=1, keepdims=True)

    def mamba_pair(i, carry):
        q, p = i // PAIRS, i % PAIRS
        rows = pl.ds(pl.multiple_of(q * TOKENS, TOKENS), TOKENS)
        lanes = pl.ds(pl.multiple_of(p * 128, 128), 128)
        xs = mamba_x[rows, lanes]
        parts, tails = [], []
        run = run_col[q]
        delta = steps[rows, :]
        for e in (0, 1):
            h = 2 * p + e
            rc = jnp.sum(jnp.where(lane16 == h, run, 0.0), axis=1, keepdims=True)
            dc = jnp.sum(jnp.where(lane16 == h, delta, 0.0), axis=1, keepdims=True)
            rr = run_row[q, pl.ds(h, 1)]
            dr = step_row[q, pl.ds(h, 1)]
            gaps = jnp.where(causal, rc - rr, NEG)
            mix = jnp.exp(gaps) * products[q] * dr
            parts.append(dot_nn(mix.astype(jnp.bfloat16), xs))
            tails.append(jnp.exp(rc[TOKENS - 1 : TOKENS] - rc) * dc)
        xf = xs.astype(jnp.float32)
        local_y[rows, lanes] = jnp.where(low_half, parts[0], parts[1]) + skip_lanes[:, lanes] * xf
        weighted = (xf * jnp.where(low_half, tails[0], tails[1])).astype(jnp.bfloat16)
        closing[i] = dot_tn(weighted, b_rows[rows, :])
        return carry

    source_row = jnp.where(row < 64, 2 * row, 2 * (row - 64) + 1)
    deal = (lane == source_row).astype(jnp.bfloat16)

    def state_head(phase):
        def step(i, carry):
            q, p = i // PAIRS, i % PAIRS
            rows = pl.ds(pl.multiple_of(q * TOKENS, TOKENS), TOKENS)
            lanes = pl.ds(pl.multiple_of(p * 128, 128), 128)
            h = 2 * p + phase
            unit = inbufs[phase][position_index[q * PER_REQUEST + MAX_PREFIX_BLOCK + p]]
            dealt = dot_nn(deal, unit)
            state = jnp.concatenate([dealt[:64], dealt[64:]], axis=1)
            rc = jnp.sum(jnp.where(lane16 == h, run_col[q], 0.0), axis=1, keepdims=True)
            blank = jnp.zeros((64, 256), jnp.bfloat16)
            sb = state.astype(jnp.bfloat16)
            both = [sb, blank] if phase == 0 else [blank, sb]
            carried = dot_nt(c_rows[rows, :], jnp.concatenate(both, axis=0))
            local_y[rows, lanes] = local_y[rows, lanes] + jnp.exp(rc) * carried
            last = jnp.exp(rc[TOKENS - 1 : TOKENS])
            final_state[q, h] = (
                last * state + closing[i, pl.ds(phase * 64, 64)]
            ).astype(jnp.bfloat16)
            return carry

        return step

    def score_group(i, carry):
        q, g = i // GROUPS, i % GROUPS
        qv = query_scr[q]
        for b in range(GROUP):
            block = g * GROUP + b
            key = kin[position_index[q * PER_REQUEST + block]]
            s = dot_nt(qv, key) * SCALING
            scores[:, pl.ds(b * 128, 128)] = jnp.where(block < counts[q], s, NEG)
        for r in range(4):
            part = pl.ds(r * TOKENS, TOKENS)
            mx = scores[part, pl.ds(0, 128)]
            for b in range(1, GROUP):
                mx = jnp.maximum(mx, scores[part, pl.ds(b * 128, 128)])
            old = top[q, part]
            m = jnp.maximum(old, jnp.max(mx, axis=1, keepdims=True))
            acc = total[q, part] * jnp.exp(old - m)
            for b in range(GROUP):
                p = jnp.exp(scores[part, pl.ds(b * 128, 128)] - m)
                acc = acc + p
                probs[i, part, pl.ds(b * 128, 128)] = p.astype(jnp.bfloat16)
            total[q, part] = acc
            top[q, part] = m
            group_top[q * (GROUPS + 1) + g, part] = m
        return carry

    def wait_in(phase):
        def step(dy, carry):
            for j in range(1, 8):
                x_copy(phase, dy, j).wait_recv()
            return carry

        lax.fori_loop(0, YN, step, 0)

    for phase in (0, 1):

        def ring_step(ss, carry, phase=phase):
            k = ss // 2 + 1
            for direction in (0, 1):
                y_copy(phase, direction, None, ss).wait_recv()

                @pl.when(ss <= 4)
                def _():
                    y_forward(phase, direction, ss).start()

                if phase == 0:

                    @pl.when(ss == 4)
                    def _():
                        y_own(1, direction, 0).start()

                    @pl.when(ss == 6)
                    def _():
                        y_own(1, direction, 1).start()

            @pl.when((ss % 2 == 1) | (ss == 6))
            def _():
                pick[...] = ybufs[phase][k - 1]
                send_chosen(phase, k)

            @pl.when(ss % 2 == 1)
            def _():
                pick[...] = ybufs[phase][YN - 1 - k]
                send_chosen(phase, YN - k)

            if phase == 0:
                lax.fori_loop(ss * 16 // 7, (ss + 1) * 16 // 7, mamba_pair, 0)
            else:

                @pl.when(ss == 0)
                def _():
                    wait_in(0)
                    lax.fori_loop(0, 16, state_head(0), 0)

                @pl.when(ss > 0)
                def _():
                    lax.fori_loop(ss * 2 - 2, ss * 2, score_group, 0)

            return carry

        lax.fori_loop(0, 7, ring_step, 0)

    for q in range(2):
        shrink = jnp.exp(group_top[q * (GROUPS + 1) + GROUPS] - top[q])
        out_acc[q] = shrink * dot_nn(suffix_probs[q], suffix_values[pl.ds(q * TOKENS, TOKENS), :])

    wait_in(1)
    lax.fori_loop(0, 16, state_head(1), 0)

    ones8 = jnp.ones((8, 128), jnp.float32)
    for q in range(2):
        rows = pl.ds(q * TOKENS, TOKENS)

        def gate_pair(p, squares, rows=rows):
            lanes = pl.ds(pl.multiple_of(p * 128, 128), 128)
            gate = mamba_gate[rows, lanes].astype(jnp.float32)
            gated = local_y[rows, lanes] * (gate / (1.0 + jnp.exp(-gate)))
            local_y[rows, lanes] = gated
            return squares + gated * gated

        squares = lax.fori_loop(0, PAIRS, gate_pair, jnp.zeros((TOKENS, 128), jnp.float32))
        square_out[q] = dot_nt(ones8, squares, HIGHEST)

    def z_copy(dz):
        return pltpu.make_async_remote_copy(
            src_ref=square_out,
            dst_ref=square_in.at[dz - 1],
            send_sem=z_send.at[dz - 1],
            recv_sem=z_recv.at[dz - 1],
            device_id=(rep, (tp + dz) % ZN),
            device_id_type=MESH,
        )

    for dz in range(1, ZN):
        z_copy(dz).start()

    def blend_group(i, carry):
        q, g = i // GROUPS, i % GROUPS
        values = [vin[position_index[q * PER_REQUEST + g * GROUP + b]] for b in range(GROUP)]
        blended = dot_nn(probs[i], jnp.concatenate(values, axis=0))
        out_acc[q] = out_acc[q] + jnp.exp(group_top[q * (GROUPS + 1) + g] - top[q]) * blended
        return carry

    lax.fori_loop(0, 2 * GROUPS, blend_group, 0)
    for q in range(2):
        for h in range(4):
            part = pl.ds(h * TOKENS, TOKENS)
            weight = jnp.sum(total[q, part], axis=1, keepdims=True)
            attn_out[pl.ds(q * TOKENS, TOKENS), pl.ds(h * 128, 128)] = (
                out_acc[q, part] / weight
            ).astype(jnp.bfloat16)

    for dz in range(1, ZN):
        z_copy(dz).wait_recv()
    unit = (row == lane).astype(jnp.float32)
    ones = jnp.ones((128, 128), jnp.float32)
    for q in range(2):
        sums = square_out[q]
        for dz in range(1, ZN):
            sums = sums + square_in[dz - 1, q]
        scale_row = lax.rsqrt(sums[0:1] / MAMBA_COLUMNS + 1e-05)
        scale = dot_nn(unit * scale_row, ones, HIGHEST)
        rows = pl.ds(q * TOKENS, TOKENS)

        def norm_pair(p, carry, rows=rows, scale=scale):
            lanes = pl.ds(pl.multiple_of(p * 128, 128), 128)
            mamba_out[rows, lanes] = (
                local_y[rows, lanes] * scale * norm_gain[:, lanes]
            ).astype(jnp.bfloat16)
            return carry

        lax.fori_loop(0, PAIRS, norm_pair, 0)

    def drain_y(ss, carry):
        for phase in (0, 1):
            for direction in (0, 1):
                y_copy(phase, direction, None, ss).wait_send()
        return carry

    def drain_x(dy, carry):
        for phase in (0, 1):
            for j in range(1, 8):
                x_copy(phase, dy, j).wait_send()
        return carry

    lax.fori_loop(0, 7, drain_y, 0)
    lax.fori_loop(0, YN, drain_x, 0)
    for dz in range(1, ZN):
        z_copy(dz).wait_send()


def tables(request_units, prefix_block_count):
    rep = lax.axis_index("rep")
    x, y, c = rep // 16, (rep // 2) % YN, rep % 2
    slot = jnp.arange(PER_REQUEST, dtype=jnp.int32)
    live = (slot[None, :] < prefix_block_count[:, None]) | (slot[None, :] >= MAX_PREFIX_BLOCK)
    owner = jnp.where(live, request_units // UNITS, -1).reshape(XN, YN, CN, POSITIONS)
    local = (request_units % UNITS).reshape(XN, YN, CN, POSITIONS)
    owner = lax.dynamic_index_in_dim(owner, y, 1, keepdims=False).reshape(XN * CN, POSITIONS)
    local = lax.dynamic_index_in_dim(local, y, 1, keepdims=False).reshape(XN * CN, POSITIONS)
    distance = jnp.arange(YN, dtype=jnp.int32)
    sources = (x * YN + (y - distance + YN) % YN) * CN + c
    ordinal = jnp.arange(POSITIONS, dtype=jnp.int32)
    code = ordinal[None, :] * UNITS + local
    hit = owner[None] == sources[:, None, None]
    first = jnp.min(jnp.where(hit, code[None], POSITIONS * UNITS), axis=2) % UNITS
    last = jnp.max(jnp.where(hit, code[None], 0), axis=2) % UNITS
    send_index = jnp.stack([first, last], axis=2).reshape(-1)
    own = lax.dynamic_index_in_dim(owner, x * CN + c, 0, keepdims=False)
    again = jnp.any(
        (own[:, None] == own[None, :]) & (ordinal[None, :] < ordinal[:, None]), axis=1
    ).astype(jnp.int32)
    ox, oy, oc = own // 16, (own // 2) % YN, own % 2
    j = ((x - ox + XN) % XN) * CN + (c - oc + CN) % CN
    position_index = (j * YN + (y - oy + YN) % YN) * 2 + again
    position_index = jnp.where(own >= 0, position_index, 0)
    counts = lax.dynamic_slice_in_dim(prefix_block_count, rep * 2, 2)
    return send_index, position_index, counts


def body(
    queries, suffix_key_rows, suffix_value_rows, mamba_input, mamba_gate, input_projection,
    output_projection, step_lengths, decay_log, skip_gain, gated_norm_gain, cache_store,
    request_units, prefix_block_count,
):
    send_index, position_index, counts = tables(request_units, prefix_block_count)
    bf16, f32 = jnp.bfloat16, jnp.float32
    vmem = pl.BlockSpec(memory_space=pltpu.VMEM)
    smem = pl.BlockSpec(memory_space=pltpu.SMEM)
    return pl.pallas_call(
        kernel,
        out_shape=(
            jax.ShapeDtypeStruct((256, 512), bf16),
            jax.ShapeDtypeStruct((256, 1024), bf16),
            jax.ShapeDtypeStruct((2, 16, 64, 256), bf16),
        ),
        in_specs=[smem] * 3 + [vmem] * 12,
        out_specs=[vmem] * 3,
        scratch_shapes=[
            pltpu.VMEM((7, UNITS, 128, 128), bf16),
            pltpu.VMEM((7, UNITS, 128, 128), bf16),
            pltpu.VMEM((UNITS, 128, 128), bf16),
            pltpu.VMEM((8, 7, 2, 128, 128), bf16),
            pltpu.VMEM((8, 7, 2, 128, 128), bf16),
            pltpu.VMEM((128, 128, 128), bf16),
            pltpu.VMEM((128, 128, 128), bf16),
            pltpu.VMEM((2 * GROUPS, ROWS, GROUP * 128), bf16),
            pltpu.VMEM((2, ROWS, 128), bf16),
            pltpu.VMEM((ROWS, GROUP * 128), f32),
            pltpu.VMEM((2, ROWS, 128), bf16),
            pltpu.VMEM((2, ROWS, 128), f32),
            pltpu.VMEM((2, ROWS, 128), f32),
            pltpu.VMEM((2 * (GROUPS + 1), ROWS, 128), f32),
            pltpu.VMEM((2, ROWS, 128), f32),
            pltpu.VMEM((2, 128, 128), f32),
            pltpu.VMEM((2, 128, 16), f32),
            pltpu.VMEM((2, 16, 128), f32),
            pltpu.VMEM((2, 16, 128), f32),
            pltpu.VMEM((256, 1024), f32),
            pltpu.VMEM((16, 128, 256), f32),
            pltpu.VMEM((2, 8, 128), f32),
            pltpu.VMEM((7, 2, 8, 128), f32),
            pltpu.SemaphoreType.DMA((28,)),
            pltpu.SemaphoreType.DMA((28,)),
            pltpu.SemaphoreType.DMA((112,)),
            pltpu.SemaphoreType.DMA((112,)),
            pltpu.SemaphoreType.DMA((7,)),
            pltpu.SemaphoreType.DMA((7,)),
        ],
        compiler_params=pltpu.CompilerParams(
            collective_id=0, has_side_effects=True, vmem_limit_bytes=62 << 20
        ),
    )(
        send_index, position_index, counts,
        queries, suffix_key_rows, suffix_value_rows, mamba_input, mamba_gate, input_projection,
        output_projection, step_lengths, decay_log[None], jnp.repeat(skip_gain, 64)[None],
        gated_norm_gain[None], cache_store.reshape(UNITS, 2, 128, 128),
    )


def solution(mesh):
    placed = (
        P("rep", "tp"),
        P("rep", "tp"),
        P("rep", "tp"),
        P("rep", "tp"),
        P("rep", "tp"),
        P("rep", None),
        P("rep", None),
        P("rep", "tp"),
        P("tp"),
        P("tp"),
        P("tp"),
        P("rep", "tp", None, None, None),
        P(),
        P(),
    )
    return jax.shard_map(
        body,
        mesh=mesh,
        in_specs=placed,
        out_specs=(P("rep", "tp"), P("rep", "tp"), P("rep", "tp", None, None)),
        check_vma=False,
    )
```

```python
import math

import jax
import jax.numpy as jnp
from jax import lax
from jax.experimental import pallas as pl
from jax.experimental.pallas import tpu as pltpu
from jax.sharding import PartitionSpec as P

MESH = pl.DeviceIdType.MESH
HEAD_WIDTH = 128
MAMBA_COLUMNS = 8192
MAX_PREFIX_BLOCK = 48
PER_REQUEST = 56
TOKENS = 128
XN, YN, CN, ZN = 4, 8, 2, 8
UNITS = 16
GROUP = 8
GROUPS = MAX_PREFIX_BLOCK // GROUP
ROWS = 512
PAIRS = 8
NEG = -1e30
HIGHEST = lax.Precision.HIGHEST
SCALING = 1.0 / math.sqrt(HEAD_WIDTH)
PARTNERS = [(dx, dc) for dx in range(XN) for dc in range(CN)]


def dot_nt(a, b, precision=None):
    return lax.dot_general(
        a, b, (((1,), (1,)), ((), ())), precision=precision, preferred_element_type=jnp.float32
    )


def dot_tn(a, b, precision=None):
    return lax.dot_general(
        a, b, (((0,), (0,)), ((), ())), precision=precision, preferred_element_type=jnp.float32
    )


def dot_nn(a, b, precision=None):
    return jnp.dot(a, b, precision=precision, preferred_element_type=jnp.float32)


def kernel(
    counts, decay_log, skip_gain, request_units, steps_row, norm_gain,
    queries_hbm, suffix_keys_hbm, suffix_values_hbm, mamba_x_hbm, mamba_gate_hbm, b_hbm, c_hbm,
    cache_hbm,
    attn_out, mamba_out, final_state,
    queries, suffix_keys, suffix_values, mamba_x, mamba_gate, b_rows, c_rows, cache,
    table_rows, table,
    yk, yv, pick, xk, xv, kin, vin, probs, suffix_probs, scores, query_scr,
    top, total, group_top, out_acc, products, run_col, step_col, run_row, step_row, local_y,
    closing, squares, square_out, square_in,
    y_send, y_recv, x_send, x_recv, z_send, z_recv, load_sem, table_sem,
):
    rep = lax.axis_index("rep")
    tp = lax.axis_index("tp")
    x, y, c = rep // 16, (rep // 2) % YN, rep % 2

    def device(dx, dy, dc):
        return (((x + dx) % XN * YN + (y + dy) % YN) * CN + (c + dc) % CN, tp)

    loads = [
        pltpu.make_async_copy(src, dst, load_sem.at[i])
        for i, (src, dst) in enumerate(
            (
                (cache_hbm, cache),
                (queries_hbm, queries),
                (suffix_keys_hbm, suffix_keys),
                (suffix_values_hbm, suffix_values),
                (b_hbm, b_rows),
                (c_hbm, c_rows),
                (mamba_x_hbm, mamba_x),
                (mamba_gate_hbm, mamba_gate),
            )
        )
    ]
    for load in loads:
        load.start()

    barrier = pltpu.get_barrier_semaphore()
    for dx, dc in PARTNERS[1:]:
        pl.semaphore_signal(barrier, 1, device_id=device(dx, 0, dc), device_id_type=MESH)
    for dy in (1, YN - 1):
        pl.semaphore_signal(barrier, 1, device_id=device(0, dy, 0), device_id_type=MESH)
    for dz in range(1, ZN):
        pl.semaphore_signal(barrier, 1, device_id=(rep, (tp + dz) % ZN), device_id_type=MESH)

    slot = lax.broadcasted_iota(jnp.int32, (PER_REQUEST, 128), 0)
    request = lax.broadcasted_iota(jnp.int32, (PER_REQUEST, 128), 1)
    request_row = request[:1]
    counts_row = jnp.zeros((1, 128), jnp.int32)
    for tx in range(XN):
        for q in range(4):
            at = tx * 32 + y * 4 + q
            counts_row = jnp.where(request_row == at, counts[at], counts_row)
    live = (slot < counts_row) | (slot >= MAX_PREFIX_BLOCK)
    units = request_units[...]
    owner = jnp.where(live, units >> 4, -1)
    code = (((request & 1) * PER_REQUEST + slot) << 4) + (units & 15)
    for dy in range(YN):
        hit = owner == (x * YN + (y + YN - dy) % YN) * CN + c
        table_rows[pl.ds(dy, 1)] = jnp.min(
            jnp.where(hit, code, 1 << 20), axis=0, keepdims=True
        )
        table_rows[pl.ds(YN + dy, 1)] = jnp.max(jnp.where(hit, code, 0), axis=0, keepdims=True)
    own_col, own_row = [], []
    for q in range(2):
        mine = jnp.where(request == rep * 2 + q, owner, 0)
        own_col.append(jnp.sum(mine, axis=1, keepdims=True))
        own_row.append(
            jnp.sum(jnp.where(slot == request, own_col[q], 0), axis=0, keepdims=True)
        )
    for q in range(2):
        same = (own_col[q] == own_row[q]) & (slot < request)
        if q == 1:
            same = same | (own_col[0] == own_row[1])
        again = jnp.max(same.astype(jnp.int32), axis=0, keepdims=True)
        ox, oy, oc = own_row[q] >> 4, (own_row[q] >> 1) & 7, own_row[q] & 1
        j = ((x - ox) & 3) * CN + ((c - oc) & 1)
        place = (j * YN + ((y - oy) & 7)) * 2 + again
        table_rows[pl.ds(2 * YN + q, 1)] = jnp.where(own_row[q] >= 0, place, 0)
    to_table = pltpu.make_async_copy(table_rows, table, table_sem)
    to_table.start()

    pl.semaphore_wait(barrier, len(PARTNERS) - 1 + 2 + ZN - 1)

    ybufs, xbufs, inbufs = (yk, yv), (xk, xv), (kin, vin)

    def y_copy(phase, direction, src, ss):
        distance, half = ss // 2 + 1, ss % 2
        row = distance - 1 if direction == 0 else YN - 1 - distance
        half = half if direction == 0 else 1 - half
        dst = ybufs[phase].at[row, pl.ds(half * 8, 8)]
        slot = (direction * 2 + phase) * 7 + ss
        return pltpu.make_async_remote_copy(
            src_ref=dst if src is None else src,
            dst_ref=dst,
            send_sem=y_send.at[slot],
            recv_sem=y_recv.at[slot],
            device_id=device(0, 1 if direction == 0 else YN - 1, 0),
            device_id_type=MESH,
        )

    def y_own(phase, direction, ss):
        half = ss if direction == 0 else 1 - ss
        return y_copy(phase, direction, cache.at[pl.ds(half * 8, 8), phase], ss)

    def y_forward(phase, direction, ss):
        distance, half = ss // 2 + 1, ss % 2
        row = distance - 1 if direction == 0 else YN - 1 - distance
        half = half if direction == 0 else 1 - half
        return y_copy(phase, direction, ybufs[phase].at[row, pl.ds(half * 8, 8)], ss + 2)

    def x_copy(phase, dy, j):
        dx, dc = PARTNERS[j]
        slot = (phase * YN + dy) * 7 + j - 1
        return pltpu.make_async_remote_copy(
            src_ref=xbufs[phase].at[dy, j - 1],
            dst_ref=inbufs[phase].at[pl.ds((j * YN + dy) * 2, 2)],
            send_sem=x_send.at[slot],
            recv_sem=x_recv.at[slot],
            device_id=device(dx, 0, dc),
            device_id_type=MESH,
        )

    def send_chosen(phase, dy):
        for j, (dx, dc) in enumerate(PARTNERS):
            at = ((x + dx) % XN) * 32 + y * 4 + ((c + dc) % CN) * 2
            first = jnp.minimum(table[dy, at], table[dy, at + 1]) & 15
            last = jnp.maximum(table[YN + dy, at], table[YN + dy, at + 1]) & 15
            for s, unit in enumerate((first, last)):
                if j == 0:
                    inbufs[phase][dy * 2 + s] = pick[unit]
                else:
                    xbufs[phase][dy, j - 1, s] = pick[unit]
            if j > 0:
                x_copy(phase, dy, j).start()

    loads[0].wait()
    for ss in (0, 1):
        for direction in (0, 1):
            y_own(0, direction, ss).start()
    to_table.wait()
    for phase in (0, 1):
        pick[...] = cache[:, phase]
        send_chosen(phase, 0)

    lane = lax.broadcasted_iota(jnp.int32, (TOKENS, 128), 1)
    row = lax.broadcasted_iota(jnp.int32, (TOKENS, 128), 0)
    low_half = lane < 64
    lane16 = lax.broadcasted_iota(jnp.int32, (TOKENS, 16), 1)
    causal = row >= lane
    for load in loads[1:]:
        load.wait()

    def rate(h):
        return -jnp.exp(jnp.full((1, 128), decay_log[h], jnp.float32))

    def place_of(q, position):
        return table[2 * YN + q, position]

    def prepare(q, carry):
        rows = pl.ds(pl.multiple_of(q * TOKENS, TOKENS), TOKENS)
        for h in range(4):
            query_scr[q, pl.ds(h * TOKENS, TOKENS)] = queries[rows, pl.ds(h * 128, 128)]
        delta = steps_row[:, rows]
        lower = (row >= lane).astype(jnp.float32)
        upper = (row <= lane).astype(jnp.float32)
        unit = (row == lane).astype(jnp.float32)
        run_col[q] = dot_nt(lower, delta, HIGHEST)
        step_col[q] = dot_nt(unit, delta, HIGHEST)
        run_row[q] = dot_nn(delta, upper, HIGHEST)
        step_row[q] = delta
        products[q] = jnp.where(causal, dot_nt(c_rows[rows, :], b_rows[rows, :]), 0.0)
        keys = suffix_keys[rows, :]
        for h in range(4):
            part = pl.ds(h * TOKENS, TOKENS)
            s = dot_nt(query_scr[q, part], keys) * SCALING
            s = jnp.where(causal, s, NEG)
            m = jnp.broadcast_to(jnp.max(s, axis=1, keepdims=True), (TOKENS, 128))
            p = jnp.exp(s - m)
            top[q, part] = m
            group_top[q * (GROUPS + 1) + GROUPS, part] = m
            total[q, part] = p
            suffix_probs[q, part] = p.astype(jnp.bfloat16)
        return carry

    lax.fori_loop(0, 2, prepare, 0)

    def column(table16, h):
        return jnp.sum(jnp.where(lane16 == h, table16, 0.0), axis=1, keepdims=True)

    def mamba_pair(i, carry):
        q, p = i // PAIRS, i % PAIRS
        rows = pl.ds(pl.multiple_of(q * TOKENS, TOKENS), TOKENS)
        lanes = pl.ds(pl.multiple_of(p * 128, 128), 128)
        xs = mamba_x[rows, lanes]
        parts, tails = [], []
        run = run_col[q]
        delta = step_col[q]
        for e in (0, 1):
            h = 2 * p + e
            rc, dc = column(run, h), column(delta, h)
            rr = run_row[q, pl.ds(h, 1)]
            dr = step_row[q, pl.ds(h, 1)]
            rh = rate(h)
            gaps = jnp.where(causal, (rc - rr) * rh, NEG)
            mix = jnp.exp(gaps) * products[q] * dr
            parts.append(dot_nn(mix.astype(jnp.bfloat16), xs))
            tails.append(jnp.exp((rc[TOKENS - 1 : TOKENS] - rc) * rh) * dc)
        xf = xs.astype(jnp.float32)
        local_y[rows, lanes] = jnp.where(
            low_half, parts[0] + skip_gain[2 * p] * xf, parts[1] + skip_gain[2 * p + 1] * xf
        )
        weighted = (xf * jnp.where(low_half, tails[0], tails[1])).astype(jnp.bfloat16)
        closing[i] = dot_tn(weighted, b_rows[rows, :])
        return carry

    source_row = jnp.where(row < 64, 2 * row, 2 * (row - 64) + 1)
    deal = (lane == source_row).astype(jnp.bfloat16)

    def state_heads(phase):
        def one(i):
            q, p = i // PAIRS, i % PAIRS
            rows = pl.ds(pl.multiple_of(q * TOKENS, TOKENS), TOKENS)
            lanes = pl.ds(pl.multiple_of(p * 128, 128), 128)
            h = 2 * p + phase
            unit = inbufs[phase][place_of(q, MAX_PREFIX_BLOCK + p)]
            dealt = dot_nn(deal, unit)
            state = jnp.concatenate([dealt[:64], dealt[64:]], axis=1)
            run = jnp.exp(column(run_col[q], h) * rate(h))
            blank = jnp.zeros((64, 256), jnp.bfloat16)
            sb = state.astype(jnp.bfloat16)
            both = [sb, blank] if phase == 0 else [blank, sb]
            carried = dot_nt(c_rows[rows, :], jnp.concatenate(both, axis=0))
            mixed = local_y[rows, lanes] + run * carried
            last = run[TOKENS - 1 : TOKENS, :1]
            final_state[q, h] = (
                last * state + closing[i, pl.ds(phase * 64, 64)]
            ).astype(jnp.bfloat16)
            if phase == 0:
                local_y[rows, lanes] = mixed
                return None
            gate = mamba_gate[rows, lanes].astype(jnp.float32)
            gated = mixed * (gate / (1.0 + jnp.exp(-gate)))
            local_y[rows, lanes] = gated
            return gated * gated

        def step(i, carry):
            found = [one(i * 4 + n) for n in range(4)]
            if phase == 1:
                squares[i] = (found[0] + found[1]) + (found[2] + found[3])
            return carry

        lax.fori_loop(0, 4, step, 0)

    def score_group(i, carry):
        q, g = i // GROUPS, i % GROUPS
        qv = query_scr[q]
        for b in range(GROUP):
            block = g * GROUP + b
            key = kin[place_of(q, block)]
            s = dot_nt(qv, key) * SCALING
            scores[:, pl.ds(b * 128, 128)] = jnp.where(block < counts[rep * 2 + q], s, NEG)
        for r in range(4):
            part = pl.ds(r * TOKENS, TOKENS)
            mx = scores[part, pl.ds(0, 128)]
            for b in range(1, GROUP):
                mx = jnp.maximum(mx, scores[part, pl.ds(b * 128, 128)])
            old = top[q, part]
            m = jnp.maximum(old, jnp.max(mx, axis=1, keepdims=True))
            acc = total[q, part] * jnp.exp(old - m)
            for b in range(GROUP):
                p = jnp.exp(scores[part, pl.ds(b * 128, 128)] - m)
                acc = acc + p
                probs[i, part, pl.ds(b * 128, 128)] = p.astype(jnp.bfloat16)
            total[q, part] = acc
            top[q, part] = m
            group_top[q * (GROUPS + 1) + g, part] = m
        return carry

    def wait_in(phase):
        def step(dy, carry):
            for j in range(1, 8):
                x_copy(phase, dy, j).wait_recv()
            return carry

        lax.fori_loop(0, YN, step, 0)

    for phase in (0, 1):

        def ring_step(ss, carry, phase=phase):
            k = ss // 2 + 1
            for direction in (0, 1):
                y_copy(phase, direction, None, ss).wait_recv()

                @pl.when(ss <= 4)
                def _():
                    y_forward(phase, direction, ss).start()

                if phase == 0:

                    @pl.when(ss == 4)
                    def _():
                        y_own(1, direction, 0).start()

                    @pl.when(ss == 6)
                    def _():
                        y_own(1, direction, 1).start()

            @pl.when((ss % 2 == 1) | (ss == 6))
            def _():
                pick[...] = ybufs[phase][k - 1]
                send_chosen(phase, k)

            @pl.when(ss % 2 == 1)
            def _():
                pick[...] = ybufs[phase][YN - 1 - k]
                send_chosen(phase, YN - k)

            if phase == 0:
                lax.fori_loop(ss * 16 // 7, (ss + 1) * 16 // 7, mamba_pair, 0)
            else:

                @pl.when(ss == 2)
                def _():
                    wait_in(0)
                    state_heads(0)

                @pl.when(ss > 2)
                def _():
                    lax.fori_loop(ss - 3, ss - 2, score_group, 0)

            return carry

        lax.fori_loop(0, 7, ring_step, 0)

    lax.fori_loop(4, 2 * GROUPS, score_group, 0)
    for q in range(2):
        shrink = jnp.exp(group_top[q * (GROUPS + 1) + GROUPS] - top[q])
        out_acc[q] = shrink * dot_nn(suffix_probs[q], suffix_values[pl.ds(q * TOKENS, TOKENS), :])

    wait_in(1)
    state_heads(1)

    ones8 = jnp.ones((8, 128), jnp.float32)
    for q in range(2):
        square_out[q] = dot_nt(ones8, squares[2 * q] + squares[2 * q + 1], HIGHEST)

    def z_copy(dz):
        return pltpu.make_async_remote_copy(
            src_ref=square_out,
            dst_ref=square_in.at[dz - 1],
            send_sem=z_send.at[dz - 1],
            recv_sem=z_recv.at[dz - 1],
            device_id=(rep, (tp + dz) % ZN),
            device_id_type=MESH,
        )

    for dz in range(1, ZN):
        z_copy(dz).start()

    def blend_group(i, carry):
        q, g = i // GROUPS, i % GROUPS
        values = [vin[place_of(q, g * GROUP + b)] for b in range(GROUP)]
        blended = dot_nn(probs[i], jnp.concatenate(values, axis=0))
        out_acc[q] = out_acc[q] + jnp.exp(group_top[q * (GROUPS + 1) + g] - top[q]) * blended
        return carry

    lax.fori_loop(0, 2 * GROUPS, blend_group, 0)
    for q in range(2):
        for h in range(4):
            part = pl.ds(h * TOKENS, TOKENS)
            weight = jnp.sum(total[q, part], axis=1, keepdims=True)
            attn_out[pl.ds(q * TOKENS, TOKENS), pl.ds(h * 128, 128)] = (
                out_acc[q, part] / weight
            ).astype(jnp.bfloat16)


    for dz in range(1, ZN):
        z_copy(dz).wait_recv()
    unit = (row == lane).astype(jnp.float32)
    ones = jnp.ones((128, 128), jnp.float32)
    for q in range(2):
        sums = square_out[q]
        for dz in range(1, ZN):
            sums = sums + square_in[dz - 1, q]
        scale_row = lax.rsqrt(sums[0:1] / MAMBA_COLUMNS + 1e-05)
        scale = dot_nn(unit * scale_row, ones, HIGHEST)
        rows = pl.ds(q * TOKENS, TOKENS)

        def norm_pair(p, carry, rows=rows, scale=scale):
            lanes = pl.ds(pl.multiple_of(p * 128, 128), 128)
            mamba_out[rows, lanes] = (
                local_y[rows, lanes] * scale * norm_gain[:, lanes]
            ).astype(jnp.bfloat16)
            return carry

        lax.fori_loop(0, PAIRS, norm_pair, 0)

    def drain_y(ss, carry):
        for phase in (0, 1):
            for direction in (0, 1):
                y_copy(phase, direction, None, ss).wait_send()
        return carry

    def drain_x(dy, carry):
        for phase in (0, 1):
            for j in range(1, 8):
                x_copy(phase, dy, j).wait_send()
        return carry

    lax.fori_loop(0, 7, drain_y, 0)
    lax.fori_loop(0, YN, drain_x, 0)
    for dz in range(1, ZN):
        z_copy(dz).wait_send()


def hand_over(*refs):
    copies = [pltpu.make_async_copy(refs[i], refs[3 + i], refs[6].at[i]) for i in range(3)]
    for copy in copies:
        copy.start()
    for copy in copies:
        copy.wait()


def body(
    queries, suffix_key_rows, suffix_value_rows, mamba_input, mamba_gate, input_projection,
    output_projection, step_lengths, decay_log, skip_gain, gated_norm_gain, cache_store,
    request_units, prefix_block_count,
):
    bf16, f32 = jnp.bfloat16, jnp.float32
    vmem = pl.BlockSpec(memory_space=pltpu.VMEM)
    smem = pl.BlockSpec(memory_space=pltpu.SMEM)
    anywhere = pl.BlockSpec(memory_space=pl.ANY)
    shapes = (
        jax.ShapeDtypeStruct((256, 512), bf16),
        jax.ShapeDtypeStruct((256, 1024), bf16),
        jax.ShapeDtypeStruct((2, 16, 64, 256), bf16),
    )
    results = pl.pallas_call(
        kernel,
        out_shape=tuple(pltpu.VMEM(s.shape, s.dtype) for s in shapes),
        in_specs=[smem] * 3 + [vmem] * 3 + [anywhere] * 8,
        out_specs=[vmem] * 3,
        scratch_shapes=[
            pltpu.VMEM((256, 512), bf16),
            pltpu.VMEM((256, 128), bf16),
            pltpu.VMEM((256, 128), bf16),
            pltpu.VMEM((256, 1024), bf16),
            pltpu.VMEM((256, 1024), bf16),
            pltpu.VMEM((256, 256), bf16),
            pltpu.VMEM((256, 256), bf16),
            pltpu.VMEM((UNITS, 2, 128, 128), bf16),
            pltpu.VMEM((24, 128), jnp.int32),
            pltpu.SMEM((24, 128), jnp.int32),
            pltpu.VMEM((7, UNITS, 128, 128), bf16),
            pltpu.VMEM((7, UNITS, 128, 128), bf16),
            pltpu.VMEM((UNITS, 128, 128), bf16),
            pltpu.VMEM((8, 7, 2, 128, 128), bf16),
            pltpu.VMEM((8, 7, 2, 128, 128), bf16),
            pltpu.VMEM((128, 128, 128), bf16),
            pltpu.VMEM((128, 128, 128), bf16),
            pltpu.VMEM((2 * GROUPS, ROWS, GROUP * 128), bf16),
            pltpu.VMEM((2, ROWS, 128), bf16),
            pltpu.VMEM((ROWS, GROUP * 128), f32),
            pltpu.VMEM((2, ROWS, 128), bf16),
            pltpu.VMEM((2, ROWS, 128), f32),
            pltpu.VMEM((2, ROWS, 128), f32),
            pltpu.VMEM((2 * (GROUPS + 1), ROWS, 128), f32),
            pltpu.VMEM((2, ROWS, 128), f32),
            pltpu.VMEM((2, 128, 128), f32),
            pltpu.VMEM((2, 128, 16), f32),
            pltpu.VMEM((2, 128, 16), f32),
            pltpu.VMEM((2, 16, 128), f32),
            pltpu.VMEM((2, 16, 128), f32),
            pltpu.VMEM((256, 1024), f32),
            pltpu.VMEM((16, 128, 256), f32),
            pltpu.VMEM((4, 128, 128), f32),
            pltpu.VMEM((2, 8, 128), f32),
            pltpu.VMEM((7, 2, 8, 128), f32),
            pltpu.SemaphoreType.DMA((28,)),
            pltpu.SemaphoreType.DMA((28,)),
            pltpu.SemaphoreType.DMA((112,)),
            pltpu.SemaphoreType.DMA((112,)),
            pltpu.SemaphoreType.DMA((7,)),
            pltpu.SemaphoreType.DMA((7,)),
            pltpu.SemaphoreType.DMA((8,)),
            pltpu.SemaphoreType.DMA,
        ],
        compiler_params=pltpu.CompilerParams(
            collective_id=0, has_side_effects=True, vmem_limit_bytes=56 << 20
        ),
    )(
        prefix_block_count, decay_log, skip_gain, request_units.T, step_lengths.T,
        gated_norm_gain[None], queries, suffix_key_rows, suffix_value_rows, mamba_input, mamba_gate,
        input_projection, output_projection, cache_store.reshape(UNITS, 2, 128, 128),
    )
    return pl.pallas_call(
        hand_over,
        out_shape=shapes,
        in_specs=[vmem] * 3,
        out_specs=[anywhere] * 3,
        scratch_shapes=[pltpu.SemaphoreType.DMA((3,))],
    )(*(pltpu.with_memory_space_constraint(r, pltpu.VMEM) for r in results))


def solution(mesh):
    placed = (
        P("rep", "tp"),
        P("rep", "tp"),
        P("rep", "tp"),
        P("rep", "tp"),
        P("rep", "tp"),
        P("rep", None),
        P("rep", None),
        P("rep", "tp"),
        P("tp"),
        P("tp"),
        P("tp"),
        P("rep", "tp", None, None, None),
        P(),
        P(),
    )
    return jax.shard_map(
        body,
        mesh=mesh,
        in_specs=placed,
        out_specs=(P("rep", "tp"), P("rep", "tp"), P("rep", "tp", None, None)),
        check_vma=False,
    )
```

```python
import math

import jax
import jax.numpy as jnp
from jax import lax
from jax.experimental import pallas as pl
from jax.experimental.pallas import tpu as pltpu
from jax.sharding import PartitionSpec as P

MESH = pl.DeviceIdType.MESH
HEAD_WIDTH = 128
MAMBA_COLUMNS = 8192
MAX_PREFIX_BLOCK = 48
PER_REQUEST = 56
TOKENS = 128
XN, YN, CN, ZN = 4, 8, 2, 8
UNITS = 16
GROUP = 8
GROUPS = MAX_PREFIX_BLOCK // GROUP
ROWS = 512
PAIRS = 8
NEG = -1e30
HIGHEST = lax.Precision.HIGHEST
SCALING = 1.0 / math.sqrt(HEAD_WIDTH)
SEND_ORDER = (0, 4, 5, 2, 3, 6, 7, 1)
PARTNERS = [(dx, dc) for dx in range(XN) for dc in range(CN)]


def dot_nt(a, b, precision=None):
    return lax.dot_general(
        a, b, (((1,), (1,)), ((), ())), precision=precision, preferred_element_type=jnp.float32
    )


def dot_tn(a, b, precision=None):
    return lax.dot_general(
        a, b, (((0,), (0,)), ((), ())), precision=precision, preferred_element_type=jnp.float32
    )


def dot_nn(a, b, precision=None):
    return jnp.dot(a, b, precision=precision, preferred_element_type=jnp.float32)


def kernel(
    counts, decay_log, skip_gain, request_units, steps_row, norm_gain,
    queries_hbm, suffix_keys_hbm, suffix_values_hbm, mamba_x_hbm, mamba_gate_hbm, b_hbm, c_hbm,
    cache_hbm,
    attn_out, mamba_out, final_state,
    queries, suffix_keys, suffix_values, mamba_x, mamba_gate, b_rows, c_rows, cache,
    table_rows, table,
    yk, yv, pick, xk, xv, kin, vin, probs, suffix_probs, scores, query_scr,
    top, total, group_top, out_acc, products, run_col, step_col, run_row, step_row, local_y,
    decay_lanes, gate_lanes,
    closing, squares, square_out, square_in,
    y_send, y_recv, x_send, x_recv, z_send, z_recv, load_sem, table_sem,
):
    rep = lax.axis_index("rep")
    tp = lax.axis_index("tp")
    x, y, c = rep // 16, (rep // 2) % YN, rep % 2

    def device(dx, dy, dc):
        return (((x + dx) % XN * YN + (y + dy) % YN) * CN + (c + dc) % CN, tp)

    barrier = pltpu.get_barrier_semaphore()
    for dx, dc in PARTNERS[1:]:
        pl.semaphore_signal(barrier, 1, device_id=device(dx, 0, dc), device_id_type=MESH)
    for dy in (1, YN - 1):
        pl.semaphore_signal(barrier, 1, device_id=device(0, dy, 0), device_id_type=MESH)
    for dz in range(1, ZN):
        pl.semaphore_signal(barrier, 1, device_id=(rep, (tp + dz) % ZN), device_id_type=MESH)

    loads = [
        pltpu.make_async_copy(src, dst, load_sem.at[i])
        for i, (src, dst) in enumerate(
            (
                (cache_hbm, cache),
                (queries_hbm, queries),
                (suffix_keys_hbm, suffix_keys),
                (suffix_values_hbm, suffix_values),
                (b_hbm, b_rows),
                (c_hbm, c_rows),
                (mamba_x_hbm, mamba_x),
                (mamba_gate_hbm, mamba_gate),
            )
        )
    ]
    for load in loads:
        load.start()

    slot = lax.broadcasted_iota(jnp.int32, (PER_REQUEST, 128), 0)
    request = lax.broadcasted_iota(jnp.int32, (PER_REQUEST, 128), 1)
    request_row = request[:1]
    counts_row = jnp.zeros((1, 128), jnp.int32)
    for tx in range(XN):
        for q in range(4):
            at = tx * 32 + y * 4 + q
            counts_row = jnp.where(request_row == at, counts[at], counts_row)
    live = (slot < counts_row) | (slot >= MAX_PREFIX_BLOCK)
    units = request_units[...]
    owner = jnp.where(live, units >> 4, -1)
    code = (((request & 1) * PER_REQUEST + slot) << 4) + (units & 15)
    for dy in range(YN):
        hit = owner == (x * YN + (y + YN - dy) % YN) * CN + c
        table_rows[pl.ds(dy, 1)] = jnp.min(
            jnp.where(hit, code, 1 << 20), axis=0, keepdims=True
        )
        table_rows[pl.ds(YN + dy, 1)] = jnp.max(jnp.where(hit, code, 0), axis=0, keepdims=True)
    own_col, own_row = [], []
    for q in range(2):
        mine = jnp.where(request == rep * 2 + q, owner, 0)
        own_col.append(jnp.sum(mine, axis=1, keepdims=True))
        own_row.append(
            jnp.sum(jnp.where(slot == request, own_col[q], 0), axis=0, keepdims=True)
        )
    for q in range(2):
        same = (own_col[q] == own_row[q]) & (slot < request)
        if q == 1:
            same = same | (own_col[0] == own_row[1])
        again = jnp.max(same.astype(jnp.int32), axis=0, keepdims=True)
        ox, oy, oc = own_row[q] >> 4, (own_row[q] >> 1) & 7, own_row[q] & 1
        j = ((x - ox) & 3) * CN + ((c - oc) & 1)
        place = (j * YN + ((y - oy) & 7)) * 2 + again
        table_rows[pl.ds(2 * YN + q, 1)] = jnp.where(own_row[q] >= 0, place, 0)
    to_table = pltpu.make_async_copy(table_rows, table, table_sem)
    to_table.start()

    pl.semaphore_wait(barrier, len(PARTNERS) - 1 + 2 + ZN - 1)

    ybufs, xbufs, inbufs = (yk, yv), (xk, xv), (kin, vin)

    def y_copy(phase, direction, src, ss):
        distance, half = ss // 2 + 1, ss % 2
        row = distance - 1 if direction == 0 else YN - 1 - distance
        half = half if direction == 0 else 1 - half
        dst = ybufs[phase].at[row, pl.ds(half * 8, 8)]
        slot = (direction * 2 + phase) * 7 + ss
        return pltpu.make_async_remote_copy(
            src_ref=dst if src is None else src,
            dst_ref=dst,
            send_sem=y_send.at[slot],
            recv_sem=y_recv.at[slot],
            device_id=device(0, 1 if direction == 0 else YN - 1, 0),
            device_id_type=MESH,
        )

    def y_own(phase, direction, ss):
        half = ss if direction == 0 else 1 - ss
        return y_copy(phase, direction, cache.at[pl.ds(half * 8, 8), phase], ss)

    def y_forward(phase, direction, ss):
        distance, half = ss // 2 + 1, ss % 2
        row = distance - 1 if direction == 0 else YN - 1 - distance
        half = half if direction == 0 else 1 - half
        return y_copy(phase, direction, ybufs[phase].at[row, pl.ds(half * 8, 8)], ss + 2)

    def x_copy(phase, dy, j):
        dx, dc = PARTNERS[j]
        slot = (phase * YN + dy) * 7 + j - 1
        return pltpu.make_async_remote_copy(
            src_ref=xbufs[phase].at[dy, j - 1],
            dst_ref=inbufs[phase].at[pl.ds((j * YN + dy) * 2, 2)],
            send_sem=x_send.at[slot],
            recv_sem=x_recv.at[slot],
            device_id=device(dx, 0, dc),
            device_id_type=MESH,
        )

    def send_chosen(phase, dy):
        for j in SEND_ORDER:
            dx, dc = PARTNERS[j]
            at = ((x + dx) % XN) * 32 + y * 4 + ((c + dc) % CN) * 2
            first = jnp.minimum(table[dy, at], table[dy, at + 1]) & 15
            last = jnp.maximum(table[YN + dy, at], table[YN + dy, at + 1]) & 15
            for s, unit in enumerate((first, last)):
                if j == 0:
                    inbufs[phase][dy * 2 + s] = pick[unit]
                else:
                    xbufs[phase][dy, j - 1, s] = pick[unit]
            if j > 0:
                x_copy(phase, dy, j).start()

    loads[0].wait()
    for ss in (0, 1):
        for direction in (0, 1):
            y_own(0, direction, ss).start()
    to_table.wait()
    for phase in (0, 1):
        pick[...] = cache[:, phase]
        send_chosen(phase, 0)

    lane = lax.broadcasted_iota(jnp.int32, (TOKENS, 128), 1)
    row = lax.broadcasted_iota(jnp.int32, (TOKENS, 128), 0)
    low_half = lane < 64
    lane16 = lax.broadcasted_iota(jnp.int32, (TOKENS, 16), 1)
    causal = row >= lane
    for load in loads[1:]:
        load.wait()

    def rate(h):
        return -jnp.exp(jnp.full((1, 128), decay_log[h], jnp.float32))

    def place_of(q, position):
        return table[2 * YN + q, position]

    def prepare(q, carry):
        rows = pl.ds(pl.multiple_of(q * TOKENS, TOKENS), TOKENS)
        for h in range(4):
            query_scr[q, pl.ds(h * TOKENS, TOKENS)] = queries[rows, pl.ds(h * 128, 128)]
        delta = steps_row[:, rows]
        lower = (row >= lane).astype(jnp.float32)
        upper = (row <= lane).astype(jnp.float32)
        unit = (row == lane).astype(jnp.float32)
        run_col[q] = dot_nt(lower, delta, HIGHEST)
        step_col[q] = dot_nt(unit, delta, HIGHEST)
        run_row[q] = dot_nn(delta, upper, HIGHEST)
        step_row[q] = delta
        products[q] = jnp.where(causal, dot_nt(c_rows[rows, :], b_rows[rows, :]), 0.0)
        keys = suffix_keys[rows, :]
        for h in range(4):
            part = pl.ds(h * TOKENS, TOKENS)
            s = dot_nt(query_scr[q, part], keys) * SCALING
            s = jnp.where(causal, s, NEG)
            m = jnp.broadcast_to(jnp.max(s, axis=1, keepdims=True), (TOKENS, 128))
            p = jnp.exp(s - m)
            top[q, part] = m
            group_top[q * (GROUPS + 1) + GROUPS, part] = m
            total[q, part] = p
            suffix_probs[q, part] = p.astype(jnp.bfloat16)
        return carry

    lax.fori_loop(0, 2, prepare, 0)

    def column(table16, h):
        return jnp.sum(jnp.where(lane16 == h, table16, 0.0), axis=1, keepdims=True)

    def mamba_pair(i, carry):
        q, p = i // PAIRS, i % PAIRS
        rows = pl.ds(pl.multiple_of(q * TOKENS, TOKENS), TOKENS)
        lanes = pl.ds(pl.multiple_of(p * 128, 128), 128)
        xs = mamba_x[rows, lanes]
        parts, tails, runs = [], [], []
        run = run_col[q]
        delta = step_col[q]
        for e in (0, 1):
            h = 2 * p + e
            rc, dc = column(run, h), column(delta, h)
            rr = run_row[q, pl.ds(h, 1)]
            dr = step_row[q, pl.ds(h, 1)]
            rh = rate(h)
            gaps = jnp.where(causal, (rc - rr) * rh, NEG)
            mix = jnp.exp(gaps) * products[q] * dr
            parts.append(dot_nn(mix.astype(jnp.bfloat16), xs))
            runs.append(rc * rh)
            tails.append(jnp.exp((rc[TOKENS - 1 : TOKENS] - rc) * rh) * dc)
        xf = xs.astype(jnp.float32)
        local_y[rows, lanes] = jnp.where(
            low_half, parts[0] + skip_gain[2 * p] * xf, parts[1] + skip_gain[2 * p + 1] * xf
        )
        weighted = (xf * jnp.where(low_half, tails[0], tails[1])).astype(jnp.bfloat16)
        closing[i] = dot_tn(weighted, b_rows[rows, :])
        decay_lanes[rows, lanes] = jnp.exp(jnp.where(low_half, runs[0], runs[1]))
        gate = mamba_gate[rows, lanes].astype(jnp.float32)
        gate_lanes[rows, lanes] = gate / (1.0 + jnp.exp(-gate))
        return carry

    source_row = jnp.where(row < 64, 2 * row, 2 * (row - 64) + 1)
    deal = (lane == source_row).astype(jnp.bfloat16)

    def state_heads(phase):
        def one(i):
            q, p = i // PAIRS, i % PAIRS
            rows = pl.ds(pl.multiple_of(q * TOKENS, TOKENS), TOKENS)
            lanes = pl.ds(pl.multiple_of(p * 128, 128), 128)
            h = 2 * p + phase
            unit = inbufs[phase][place_of(q, MAX_PREFIX_BLOCK + p)]
            dealt = dot_nn(deal, unit)
            state = jnp.concatenate([dealt[:64], dealt[64:]], axis=1)
            run = decay_lanes[rows, lanes]
            blank = jnp.zeros((64, 256), jnp.bfloat16)
            sb = state.astype(jnp.bfloat16)
            both = [sb, blank] if phase == 0 else [blank, sb]
            carried = dot_nt(c_rows[rows, :], jnp.concatenate(both, axis=0))
            mixed = local_y[rows, lanes] + run * carried
            last = run[TOKENS - 1 : TOKENS, phase * 64 : phase * 64 + 1]
            final_state[q, h] = (
                last * state + closing[i, pl.ds(phase * 64, 64)]
            ).astype(jnp.bfloat16)
            if phase == 0:
                local_y[rows, lanes] = mixed
                return None
            gated = mixed * gate_lanes[rows, lanes]
            local_y[rows, lanes] = gated
            return gated * gated

        def step(i, carry):
            found = [one(i * 4 + n) for n in range(4)]
            if phase == 1:
                squares[i] = (found[0] + found[1]) + (found[2] + found[3])
            return carry

        lax.fori_loop(0, 4, step, 0)

    def score_group(i, carry):
        q, g = i // GROUPS, i % GROUPS
        qv = query_scr[q]
        for b in range(GROUP):
            block = g * GROUP + b
            key = kin[place_of(q, block)]
            s = dot_nt(qv, key) * SCALING
            scores[:, pl.ds(b * 128, 128)] = jnp.where(block < counts[rep * 2 + q], s, NEG)
        for r in range(4):
            part = pl.ds(r * TOKENS, TOKENS)
            mx = scores[part, pl.ds(0, 128)]
            for b in range(1, GROUP):
                mx = jnp.maximum(mx, scores[part, pl.ds(b * 128, 128)])
            old = top[q, part]
            m = jnp.maximum(old, jnp.max(mx, axis=1, keepdims=True))
            acc = total[q, part] * jnp.exp(old - m)
            for b in range(GROUP):
                p = jnp.exp(scores[part, pl.ds(b * 128, 128)] - m)
                acc = acc + p
                probs[i, part, pl.ds(b * 128, 128)] = p.astype(jnp.bfloat16)
            total[q, part] = acc
            top[q, part] = m
            group_top[q * (GROUPS + 1) + g, part] = m
        return carry

    def wait_in(phase):
        def step(dy, carry):
            for j in range(1, 8):
                x_copy(phase, dy, j).wait_recv()
            return carry

        lax.fori_loop(0, YN, step, 0)

    for phase in (0, 1):

        def ring_step(ss, carry, phase=phase):
            k = ss // 2 + 1
            for direction in (0, 1):
                y_copy(phase, direction, None, ss).wait_recv()

                @pl.when(ss <= 4)
                def _():
                    y_forward(phase, direction, ss).start()

                if phase == 0:

                    @pl.when(ss == 4)
                    def _():
                        y_own(1, direction, 0).start()

                    @pl.when(ss == 6)
                    def _():
                        y_own(1, direction, 1).start()

            @pl.when((ss % 2 == 1) | (ss == 6))
            def _():
                pick[...] = ybufs[phase][k - 1]
                send_chosen(phase, k)

            @pl.when(ss % 2 == 1)
            def _():
                pick[...] = ybufs[phase][YN - 1 - k]
                send_chosen(phase, YN - k)

            if phase == 0:
                lax.fori_loop(ss * 16 // 7, (ss + 1) * 16 // 7, mamba_pair, 0)
            else:

                @pl.when(ss == 3)
                def _():
                    wait_in(0)
                    state_heads(0)

                @pl.when((ss == 4) | (ss == 5))
                def _():
                    lax.fori_loop(ss * 2 - 8, ss * 2 - 6, score_group, 0)

            return carry

        lax.fori_loop(0, 7, ring_step, 0)

    lax.fori_loop(4, 2 * GROUPS, score_group, 0)
    for q in range(2):
        shrink = jnp.exp(group_top[q * (GROUPS + 1) + GROUPS] - top[q])
        out_acc[q] = shrink * dot_nn(suffix_probs[q], suffix_values[pl.ds(q * TOKENS, TOKENS), :])

    wait_in(1)
    state_heads(1)

    ones8 = jnp.ones((8, 128), jnp.float32)
    for q in range(2):
        square_out[q] = dot_nt(ones8, squares[2 * q] + squares[2 * q + 1], HIGHEST)

    def z_copy(dz):
        return pltpu.make_async_remote_copy(
            src_ref=square_out,
            dst_ref=square_in.at[dz - 1],
            send_sem=z_send.at[dz - 1],
            recv_sem=z_recv.at[dz - 1],
            device_id=(rep, (tp + dz) % ZN),
            device_id_type=MESH,
        )

    for dz in range(1, ZN):
        z_copy(dz).start()

    def blend_group(i, carry):
        q, g = i // GROUPS, i % GROUPS
        values = [vin[place_of(q, g * GROUP + b)] for b in range(GROUP)]
        blended = dot_nn(probs[i], jnp.concatenate(values, axis=0))
        out_acc[q] = out_acc[q] + jnp.exp(group_top[q * (GROUPS + 1) + g] - top[q]) * blended
        return carry

    lax.fori_loop(0, 2 * GROUPS, blend_group, 0)
    for q in range(2):
        for h in range(4):
            part = pl.ds(h * TOKENS, TOKENS)
            weight = jnp.sum(total[q, part], axis=1, keepdims=True)
            attn_out[pl.ds(q * TOKENS, TOKENS), pl.ds(h * 128, 128)] = (
                out_acc[q, part] / weight
            ).astype(jnp.bfloat16)


    for dz in range(1, ZN):
        z_copy(dz).wait_recv()
    unit = (row == lane).astype(jnp.float32)
    ones = jnp.ones((128, 128), jnp.float32)
    for q in range(2):
        sums = square_out[q]
        for dz in range(1, ZN):
            sums = sums + square_in[dz - 1, q]
        scale_row = lax.rsqrt(sums[0:1] / MAMBA_COLUMNS + 1e-05)
        scale = dot_nn(unit * scale_row, ones, HIGHEST)
        rows = pl.ds(q * TOKENS, TOKENS)

        def norm_pair(p, carry, rows=rows, scale=scale):
            lanes = pl.ds(pl.multiple_of(p * 128, 128), 128)
            mamba_out[rows, lanes] = (
                local_y[rows, lanes] * scale * norm_gain[:, lanes]
            ).astype(jnp.bfloat16)
            return carry

        lax.fori_loop(0, PAIRS, norm_pair, 0)

    def drain_y(ss, carry):
        for phase in (0, 1):
            for direction in (0, 1):
                y_copy(phase, direction, None, ss).wait_send()
        return carry

    def drain_x(dy, carry):
        for phase in (0, 1):
            for j in range(1, 8):
                x_copy(phase, dy, j).wait_send()
        return carry

    lax.fori_loop(0, 7, drain_y, 0)
    lax.fori_loop(0, YN, drain_x, 0)
    for dz in range(1, ZN):
        z_copy(dz).wait_send()


def hand_over(*refs):
    copies = [pltpu.make_async_copy(refs[i], refs[3 + i], refs[6].at[i]) for i in range(3)]
    for copy in copies:
        copy.start()
    for copy in copies:
        copy.wait()


def body(
    queries, suffix_key_rows, suffix_value_rows, mamba_input, mamba_gate, input_projection,
    output_projection, step_lengths, decay_log, skip_gain, gated_norm_gain, cache_store,
    request_units, prefix_block_count,
):
    bf16, f32 = jnp.bfloat16, jnp.float32
    vmem = pl.BlockSpec(memory_space=pltpu.VMEM)
    smem = pl.BlockSpec(memory_space=pltpu.SMEM)
    anywhere = pl.BlockSpec(memory_space=pl.ANY)
    shapes = (
        jax.ShapeDtypeStruct((256, 512), bf16),
        jax.ShapeDtypeStruct((256, 1024), bf16),
        jax.ShapeDtypeStruct((2, 16, 64, 256), bf16),
    )
    results = pl.pallas_call(
        kernel,
        out_shape=tuple(pltpu.VMEM(s.shape, s.dtype) for s in shapes),
        in_specs=[smem] * 3 + [vmem] * 3 + [anywhere] * 8,
        out_specs=[vmem] * 3,
        scratch_shapes=[
            pltpu.VMEM((256, 512), bf16),
            pltpu.VMEM((256, 128), bf16),
            pltpu.VMEM((256, 128), bf16),
            pltpu.VMEM((256, 1024), bf16),
            pltpu.VMEM((256, 1024), bf16),
            pltpu.VMEM((256, 256), bf16),
            pltpu.VMEM((256, 256), bf16),
            pltpu.VMEM((UNITS, 2, 128, 128), bf16),
            pltpu.VMEM((24, 128), jnp.int32),
            pltpu.SMEM((24, 128), jnp.int32),
            pltpu.VMEM((7, UNITS, 128, 128), bf16),
            pltpu.VMEM((7, UNITS, 128, 128), bf16),
            pltpu.VMEM((UNITS, 128, 128), bf16),
            pltpu.VMEM((8, 7, 2, 128, 128), bf16),
            pltpu.VMEM((8, 7, 2, 128, 128), bf16),
            pltpu.VMEM((128, 128, 128), bf16),
            pltpu.VMEM((128, 128, 128), bf16),
            pltpu.VMEM((2 * GROUPS, ROWS, GROUP * 128), bf16),
            pltpu.VMEM((2, ROWS, 128), bf16),
            pltpu.VMEM((ROWS, GROUP * 128), f32),
            pltpu.VMEM((2, ROWS, 128), bf16),
            pltpu.VMEM((2, ROWS, 128), f32),
            pltpu.VMEM((2, ROWS, 128), f32),
            pltpu.VMEM((2 * (GROUPS + 1), ROWS, 128), f32),
            pltpu.VMEM((2, ROWS, 128), f32),
            pltpu.VMEM((2, 128, 128), f32),
            pltpu.VMEM((2, 128, 16), f32),
            pltpu.VMEM((2, 128, 16), f32),
            pltpu.VMEM((2, 16, 128), f32),
            pltpu.VMEM((2, 16, 128), f32),
            pltpu.VMEM((256, 1024), f32),
            pltpu.VMEM((256, 1024), f32),
            pltpu.VMEM((256, 1024), f32),
            pltpu.VMEM((16, 128, 256), f32),
            pltpu.VMEM((4, 128, 128), f32),
            pltpu.VMEM((2, 8, 128), f32),
            pltpu.VMEM((7, 2, 8, 128), f32),
            pltpu.SemaphoreType.DMA((28,)),
            pltpu.SemaphoreType.DMA((28,)),
            pltpu.SemaphoreType.DMA((112,)),
            pltpu.SemaphoreType.DMA((112,)),
            pltpu.SemaphoreType.DMA((7,)),
            pltpu.SemaphoreType.DMA((7,)),
            pltpu.SemaphoreType.DMA((8,)),
            pltpu.SemaphoreType.DMA,
        ],
        compiler_params=pltpu.CompilerParams(
            collective_id=0, has_side_effects=True, vmem_limit_bytes=56 << 20
        ),
    )(
        prefix_block_count, decay_log, skip_gain, request_units.T, step_lengths.T,
        gated_norm_gain[None], queries, suffix_key_rows, suffix_value_rows, mamba_input, mamba_gate,
        input_projection, output_projection, cache_store.reshape(UNITS, 2, 128, 128),
    )
    return pl.pallas_call(
        hand_over,
        out_shape=shapes,
        in_specs=[vmem] * 3,
        out_specs=[anywhere] * 3,
        scratch_shapes=[pltpu.SemaphoreType.DMA((3,))],
    )(*(pltpu.with_memory_space_constraint(r, pltpu.VMEM) for r in results))


def solution(mesh):
    placed = (
        P("rep", "tp"),
        P("rep", "tp"),
        P("rep", "tp"),
        P("rep", "tp"),
        P("rep", "tp"),
        P("rep", None),
        P("rep", None),
        P("rep", "tp"),
        P("tp"),
        P("tp"),
        P("tp"),
        P("rep", "tp", None, None, None),
        P(),
        P(),
    )
    return jax.shard_map(
        body,
        mesh=mesh,
        in_specs=placed,
        out_specs=(P("rep", "tp"), P("rep", "tp"), P("rep", "tp", None, None)),
        check_vma=False,
    )
```

```python
import math

import jax
import jax.numpy as jnp
from jax import lax
from jax.experimental import pallas as pl
from jax.experimental.pallas import tpu as pltpu
from jax.sharding import PartitionSpec as P

MESH = pl.DeviceIdType.MESH
HEAD_WIDTH = 128
MAMBA_COLUMNS = 8192
MAX_PREFIX_BLOCK = 48
PER_REQUEST = 56
TOKENS = 128
XN, YN, CN, ZN = 4, 8, 2, 8
UNITS = 16
GROUP = 8
GROUPS = MAX_PREFIX_BLOCK // GROUP
ROWS = 512
PAIRS = 8
NEG = -1e30
HIGHEST = lax.Precision.HIGHEST
SCALING = 1.0 / math.sqrt(HEAD_WIDTH)
SEND_ORDER = (0, 4, 5, 2, 3, 6, 7, 1)
PARTNERS = [(dx, dc) for dx in range(XN) for dc in range(CN)]


def dot_nt(a, b, precision=None):
    return lax.dot_general(
        a, b, (((1,), (1,)), ((), ())), precision=precision, preferred_element_type=jnp.float32
    )


def dot_tn(a, b, precision=None):
    return lax.dot_general(
        a, b, (((0,), (0,)), ((), ())), precision=precision, preferred_element_type=jnp.float32
    )


def dot_nn(a, b, precision=None):
    return jnp.dot(a, b, precision=precision, preferred_element_type=jnp.float32)


def kernel(
    counts, decay_log, skip_gain, request_units, steps_row, norm_gain,
    queries_hbm, suffix_keys_hbm, suffix_values_hbm, mamba_x_hbm, mamba_gate_hbm, b_hbm, c_hbm,
    cache_hbm,
    attn_out, mamba_out, final_state,
    queries, suffix_keys, suffix_values, mamba_x, mamba_gate, b_rows, c_rows, cache,
    table_rows, table,
    yk, yv, pick, xk, xv, kin, vin, probs, suffix_probs, scores, query_scr,
    top, total, group_top, out_acc, products, run_col, step_col, run_row, step_row, local_y,
    decay_lanes, gate_lanes,
    closing, squares, square_out, square_in,
    y_send, y_recv, x_send, x_recv, z_send, z_recv, load_sem, table_sem,
):
    rep = lax.axis_index("rep")
    tp = lax.axis_index("tp")
    x, y, c = rep // 16, (rep // 2) % YN, rep % 2

    def device(dx, dy, dc):
        return (((x + dx) % XN * YN + (y + dy) % YN) * CN + (c + dc) % CN, tp)

    barrier = pltpu.get_barrier_semaphore()
    for dx, dc in PARTNERS[1:]:
        pl.semaphore_signal(barrier, 1, device_id=device(dx, 0, dc), device_id_type=MESH)
    for dy in (1, YN - 1):
        pl.semaphore_signal(barrier, 1, device_id=device(0, dy, 0), device_id_type=MESH)
    for dz in range(1, ZN):
        pl.semaphore_signal(barrier, 1, device_id=(rep, (tp + dz) % ZN), device_id_type=MESH)

    loads = [
        pltpu.make_async_copy(src, dst, load_sem.at[i])
        for i, (src, dst) in enumerate(
            (
                (cache_hbm, cache),
                (queries_hbm, queries),
                (suffix_keys_hbm, suffix_keys),
                (suffix_values_hbm, suffix_values),
                (b_hbm, b_rows),
                (c_hbm, c_rows),
                (mamba_x_hbm, mamba_x),
                (mamba_gate_hbm, mamba_gate),
            )
        )
    ]
    for load in loads:
        load.start()

    slot = lax.broadcasted_iota(jnp.int32, (PER_REQUEST, 128), 0)
    request = lax.broadcasted_iota(jnp.int32, (PER_REQUEST, 128), 1)
    request_row = request[:1]
    counts_row = jnp.zeros((1, 128), jnp.int32)
    for tx in range(XN):
        for q in range(4):
            at = tx * 32 + y * 4 + q
            counts_row = jnp.where(request_row == at, counts[at], counts_row)
    live = (slot < counts_row) | (slot >= MAX_PREFIX_BLOCK)
    units = request_units[...]
    owner = jnp.where(live, units >> 4, -1)
    code = (((request & 1) * PER_REQUEST + slot) << 4) + (units & 15)
    for dy in range(YN):
        hit = owner == (x * YN + (y + YN - dy) % YN) * CN + c
        table_rows[pl.ds(dy, 1)] = jnp.min(
            jnp.where(hit, code, 1 << 20), axis=0, keepdims=True
        )
        table_rows[pl.ds(YN + dy, 1)] = jnp.max(jnp.where(hit, code, 0), axis=0, keepdims=True)
    own_col, own_row = [], []
    for q in range(2):
        mine = jnp.where(request == rep * 2 + q, owner, 0)
        own_col.append(jnp.sum(mine, axis=1, keepdims=True))
        own_row.append(
            jnp.sum(jnp.where(slot == request, own_col[q], 0), axis=0, keepdims=True)
        )
    for q in range(2):
        same = (own_col[q] == own_row[q]) & (slot < request)
        if q == 1:
            same = same | (own_col[0] == own_row[1])
        again = jnp.max(same.astype(jnp.int32), axis=0, keepdims=True)
        ox, oy, oc = own_row[q] >> 4, (own_row[q] >> 1) & 7, own_row[q] & 1
        j = ((x - ox) & 3) * CN + ((c - oc) & 1)
        dy = (y - oy) & 7
        chunk = jnp.where(dy < 4, 2 * dy, jnp.where(dy == 4, 1, 2 * (YN - dy) + 1))
        place = (j * YN + chunk) * 2 + again
        table_rows[pl.ds(2 * YN + q, 1)] = jnp.where(own_row[q] >= 0, place, 0)
    to_table = pltpu.make_async_copy(table_rows, table, table_sem)
    to_table.start()

    pl.semaphore_wait(barrier, len(PARTNERS) - 1 + 2 + ZN - 1)

    ybufs, xbufs, inbufs = (yk, yv), (xk, xv), (kin, vin)

    def y_copy(phase, direction, src, ss):
        distance, half = ss // 2 + 1, ss % 2
        row = distance - 1 if direction == 0 else YN - 1 - distance
        half = half if direction == 0 else 1 - half
        dst = ybufs[phase].at[row, pl.ds(half * 8, 8)]
        slot = (direction * 2 + phase) * 7 + ss
        return pltpu.make_async_remote_copy(
            src_ref=dst if src is None else src,
            dst_ref=dst,
            send_sem=y_send.at[slot],
            recv_sem=y_recv.at[slot],
            device_id=device(0, 1 if direction == 0 else YN - 1, 0),
            device_id_type=MESH,
        )

    def y_own(phase, direction, ss):
        half = ss if direction == 0 else 1 - ss
        return y_copy(phase, direction, cache.at[pl.ds(half * 8, 8), phase], ss)

    def y_forward(phase, direction, ss):
        distance, half = ss // 2 + 1, ss % 2
        row = distance - 1 if direction == 0 else YN - 1 - distance
        half = half if direction == 0 else 1 - half
        return y_copy(phase, direction, ybufs[phase].at[row, pl.ds(half * 8, 8)], ss + 2)

    def x_copy(phase, at, j, chunks):
        dx, dc = PARTNERS[j]
        slot = (phase * YN + at) * 7 + j - 1
        return pltpu.make_async_remote_copy(
            src_ref=xbufs[phase].at[j - 1, pl.ds(at * 2, 2 * chunks)],
            dst_ref=inbufs[phase].at[pl.ds((j * YN + at) * 2, 2 * chunks)],
            send_sem=x_send.at[slot],
            recv_sem=x_recv.at[slot],
            device_id=device(dx, 0, dc),
            device_id_type=MESH,
        )

    def choose(phase, dy, place):
        for j in SEND_ORDER:
            dx, dc = PARTNERS[j]
            at = ((x + dx) % XN) * 32 + y * 4 + ((c + dc) % CN) * 2
            first = jnp.minimum(table[dy, at], table[dy, at + 1]) & 15
            last = jnp.maximum(table[YN + dy, at], table[YN + dy, at + 1]) & 15
            for s, unit in enumerate((first, last)):
                if j == 0:
                    inbufs[phase][place * 2 + s] = pick[unit]
                else:
                    xbufs[phase][j - 1, place * 2 + s] = pick[unit]

    def send(phase, place, chunks):
        for j in SEND_ORDER[1:]:
            x_copy(phase, place, j, chunks).start()

    loads[0].wait()
    for ss in (0, 1):
        for direction in (0, 1):
            y_own(0, direction, ss).start()
    to_table.wait()
    for phase in (0, 1):
        pick[...] = cache[:, phase]
        choose(phase, 0, 0)
        send(phase, 0, 1)

    lane = lax.broadcasted_iota(jnp.int32, (TOKENS, 128), 1)
    row = lax.broadcasted_iota(jnp.int32, (TOKENS, 128), 0)
    low_half = lane < 64
    lane16 = lax.broadcasted_iota(jnp.int32, (TOKENS, 16), 1)
    causal = row >= lane
    for load in loads[1:]:
        load.wait()

    def rate(h):
        return -jnp.exp(jnp.full((1, 128), decay_log[h], jnp.float32))

    def place_of(q, position):
        return table[2 * YN + q, position]

    def prepare(q, carry):
        rows = pl.ds(pl.multiple_of(q * TOKENS, TOKENS), TOKENS)
        for h in range(4):
            query_scr[q, pl.ds(h * TOKENS, TOKENS)] = queries[rows, pl.ds(h * 128, 128)]
        delta = steps_row[:, rows]
        lower = (row >= lane).astype(jnp.float32)
        upper = (row <= lane).astype(jnp.float32)
        unit = (row == lane).astype(jnp.float32)
        run_col[q] = dot_nt(lower, delta, HIGHEST)
        step_col[q] = dot_nt(unit, delta, HIGHEST)
        run_row[q] = dot_nn(delta, upper, HIGHEST)
        step_row[q] = delta
        products[q] = jnp.where(causal, dot_nt(c_rows[rows, :], b_rows[rows, :]), 0.0)
        keys = suffix_keys[rows, :]
        for h in range(4):
            part = pl.ds(h * TOKENS, TOKENS)
            s = dot_nt(query_scr[q, part], keys) * SCALING
            s = jnp.where(causal, s, NEG)
            m = jnp.broadcast_to(jnp.max(s, axis=1, keepdims=True), (TOKENS, 128))
            p = jnp.exp(s - m)
            top[q, part] = m
            group_top[q * (GROUPS + 1) + GROUPS, part] = m
            total[q, part] = p
            suffix_probs[q, part] = p.astype(jnp.bfloat16)
        return carry

    lax.fori_loop(0, 2, prepare, 0)

    def column(table16, h):
        return jnp.sum(jnp.where(lane16 == h, table16, 0.0), axis=1, keepdims=True)

    def mamba_pair(i, carry):
        q, p = i // PAIRS, i % PAIRS
        rows = pl.ds(pl.multiple_of(q * TOKENS, TOKENS), TOKENS)
        lanes = pl.ds(pl.multiple_of(p * 128, 128), 128)
        xs = mamba_x[rows, lanes]
        parts, tails, runs = [], [], []
        run = run_col[q]
        delta = step_col[q]
        for e in (0, 1):
            h = 2 * p + e
            rc, dc = column(run, h), column(delta, h)
            rr = run_row[q, pl.ds(h, 1)]
            dr = step_row[q, pl.ds(h, 1)]
            rh = rate(h)
            gaps = jnp.where(causal, (rc - rr) * rh, NEG)
            mix = jnp.exp(gaps) * products[q] * dr
            parts.append(dot_nn(mix.astype(jnp.bfloat16), xs))
            runs.append(rc * rh)
            tails.append(jnp.exp((rc[TOKENS - 1 : TOKENS] - rc) * rh) * dc)
        xf = xs.astype(jnp.float32)
        local_y[rows, lanes] = jnp.where(
            low_half, parts[0] + skip_gain[2 * p] * xf, parts[1] + skip_gain[2 * p + 1] * xf
        )
        weighted = (xf * jnp.where(low_half, tails[0], tails[1])).astype(jnp.bfloat16)
        closing[i] = dot_tn(weighted, b_rows[rows, :])
        decay_lanes[rows, lanes] = jnp.exp(jnp.where(low_half, runs[0], runs[1]))
        gate = mamba_gate[rows, lanes].astype(jnp.float32)
        gate_lanes[rows, lanes] = gate / (1.0 + jnp.exp(-gate))
        return carry

    source_row = jnp.where(row < 64, 2 * row, 2 * (row - 64) + 1)
    deal = (lane == source_row).astype(jnp.bfloat16)

    def state_heads(phase):
        def one(i):
            q, p = i // PAIRS, i % PAIRS
            rows = pl.ds(pl.multiple_of(q * TOKENS, TOKENS), TOKENS)
            lanes = pl.ds(pl.multiple_of(p * 128, 128), 128)
            h = 2 * p + phase
            unit = inbufs[phase][place_of(q, MAX_PREFIX_BLOCK + p)]
            dealt = dot_nn(deal, unit)
            state = jnp.concatenate([dealt[:64], dealt[64:]], axis=1)
            run = decay_lanes[rows, lanes]
            blank = jnp.zeros((64, 256), jnp.bfloat16)
            sb = state.astype(jnp.bfloat16)
            both = [sb, blank] if phase == 0 else [blank, sb]
            carried = dot_nt(c_rows[rows, :], jnp.concatenate(both, axis=0))
            mixed = local_y[rows, lanes] + run * carried
            last = run[TOKENS - 1 : TOKENS, phase * 64 : phase * 64 + 1]
            final_state[q, h] = (
                last * state + closing[i, pl.ds(phase * 64, 64)]
            ).astype(jnp.bfloat16)
            if phase == 0:
                local_y[rows, lanes] = mixed
                return None
            gated = mixed * gate_lanes[rows, lanes]
            local_y[rows, lanes] = gated
            return gated * gated

        def step(i, carry):
            found = [one(i * 4 + n) for n in range(4)]
            if phase == 1:
                squares[i] = (found[0] + found[1]) + (found[2] + found[3])
            return carry

        lax.fori_loop(0, 4, step, 0)

    def score_group(i, carry):
        q, g = i // GROUPS, i % GROUPS
        qv = query_scr[q]
        for b in range(GROUP):
            block = g * GROUP + b
            key = kin[place_of(q, block)]
            s = dot_nt(qv, key) * SCALING
            scores[:, pl.ds(b * 128, 128)] = jnp.where(block < counts[rep * 2 + q], s, NEG)
        for r in range(4):
            part = pl.ds(r * TOKENS, TOKENS)
            mx = scores[part, pl.ds(0, 128)]
            for b in range(1, GROUP):
                mx = jnp.maximum(mx, scores[part, pl.ds(b * 128, 128)])
            old = top[q, part]
            m = jnp.maximum(old, jnp.max(mx, axis=1, keepdims=True))
            acc = total[q, part] * jnp.exp(old - m)
            for b in range(GROUP):
                p = jnp.exp(scores[part, pl.ds(b * 128, 128)] - m)
                acc = acc + p
                probs[i, part, pl.ds(b * 128, 128)] = p.astype(jnp.bfloat16)
            total[q, part] = acc
            top[q, part] = m
            group_top[q * (GROUPS + 1) + g, part] = m
        return carry

    def wait_in(phase):
        def step(k, carry):
            for j in range(1, 8):
                x_copy(phase, 2 * k, j, 2).wait_recv()
            return carry

        for j in range(1, 8):
            x_copy(phase, 0, j, 1).wait_recv()
            x_copy(phase, 1, j, 1).wait_recv()
        lax.fori_loop(1, 4, step, 0)

    for phase in (0, 1):

        def ring_step(ss, carry, phase=phase):
            k = ss // 2 + 1
            for direction in (0, 1):
                y_copy(phase, direction, None, ss).wait_recv()

                @pl.when(ss <= 4)
                def _():
                    y_forward(phase, direction, ss).start()

                if phase == 0:

                    @pl.when(ss == 4)
                    def _():
                        y_own(1, direction, 0).start()

                    @pl.when(ss == 6)
                    def _():
                        y_own(1, direction, 1).start()

            @pl.when(ss == 6)
            def _():
                pick[...] = ybufs[phase][3]
                choose(phase, 4, 1)
                send(phase, 1, 1)

            @pl.when(ss % 2 == 1)
            def _():
                pick[...] = ybufs[phase][k - 1]
                choose(phase, k, 2 * k)
                pick[...] = ybufs[phase][YN - 1 - k]
                choose(phase, YN - k, 2 * k + 1)
                send(phase, 2 * k, 2)

            if phase == 0:
                lax.fori_loop(ss * 16 // 7, (ss + 1) * 16 // 7, mamba_pair, 0)
            else:

                @pl.when(ss == 3)
                def _():
                    wait_in(0)
                    state_heads(0)

                @pl.when((ss == 4) | (ss == 5))
                def _():
                    lax.fori_loop(ss * 2 - 8, ss * 2 - 6, score_group, 0)

            return carry

        lax.fori_loop(0, 7, ring_step, 0)

    lax.fori_loop(4, 2 * GROUPS, score_group, 0)
    for q in range(2):
        shrink = jnp.exp(group_top[q * (GROUPS + 1) + GROUPS] - top[q])
        out_acc[q] = shrink * dot_nn(suffix_probs[q], suffix_values[pl.ds(q * TOKENS, TOKENS), :])

    wait_in(1)
    state_heads(1)

    ones8 = jnp.ones((8, 128), jnp.float32)
    for q in range(2):
        square_out[q] = dot_nt(ones8, squares[2 * q] + squares[2 * q + 1], HIGHEST)

    def z_copy(dz):
        return pltpu.make_async_remote_copy(
            src_ref=square_out,
            dst_ref=square_in.at[dz - 1],
            send_sem=z_send.at[dz - 1],
            recv_sem=z_recv.at[dz - 1],
            device_id=(rep, (tp + dz) % ZN),
            device_id_type=MESH,
        )

    for dz in range(1, ZN):
        z_copy(dz).start()

    def blend_group(i, carry):
        q, g = i // GROUPS, i % GROUPS
        values = [vin[place_of(q, g * GROUP + b)] for b in range(GROUP)]
        blended = dot_nn(probs[i], jnp.concatenate(values, axis=0))
        out_acc[q] = out_acc[q] + jnp.exp(group_top[q * (GROUPS + 1) + g] - top[q]) * blended
        return carry

    lax.fori_loop(0, 2 * GROUPS, blend_group, 0)
    for q in range(2):
        for h in range(4):
            part = pl.ds(h * TOKENS, TOKENS)
            weight = jnp.sum(total[q, part], axis=1, keepdims=True)
            attn_out[pl.ds(q * TOKENS, TOKENS), pl.ds(h * 128, 128)] = (
                out_acc[q, part] / weight
            ).astype(jnp.bfloat16)


    for dz in range(1, ZN):
        z_copy(dz).wait_recv()
    unit = (row == lane).astype(jnp.float32)
    ones = jnp.ones((128, 128), jnp.float32)
    for q in range(2):
        sums = square_out[q]
        for dz in range(1, ZN):
            sums = sums + square_in[dz - 1, q]
        scale_row = lax.rsqrt(sums[0:1] / MAMBA_COLUMNS + 1e-05)
        scale = dot_nn(unit * scale_row, ones, HIGHEST)
        rows = pl.ds(q * TOKENS, TOKENS)

        def norm_pair(p, carry, rows=rows, scale=scale):
            lanes = pl.ds(pl.multiple_of(p * 128, 128), 128)
            mamba_out[rows, lanes] = (
                local_y[rows, lanes] * scale * norm_gain[:, lanes]
            ).astype(jnp.bfloat16)
            return carry

        lax.fori_loop(0, PAIRS, norm_pair, 0)

    def drain_y(ss, carry):
        for phase in (0, 1):
            for direction in (0, 1):
                y_copy(phase, direction, None, ss).wait_send()
        return carry

    def drain_x(k, carry):
        for phase in (0, 1):
            for j in range(1, 8):
                x_copy(phase, 2 * k, j, 2).wait_send()
        return carry

    lax.fori_loop(0, 7, drain_y, 0)
    for phase in (0, 1):
        for j in range(1, 8):
            x_copy(phase, 0, j, 1).wait_send()
            x_copy(phase, 1, j, 1).wait_send()
    lax.fori_loop(1, 4, drain_x, 0)
    for dz in range(1, ZN):
        z_copy(dz).wait_send()


def hand_over(*refs):
    copies = [pltpu.make_async_copy(refs[i], refs[3 + i], refs[6].at[i]) for i in range(3)]
    for copy in copies:
        copy.start()
    for copy in copies:
        copy.wait()


def body(
    queries, suffix_key_rows, suffix_value_rows, mamba_input, mamba_gate, input_projection,
    output_projection, step_lengths, decay_log, skip_gain, gated_norm_gain, cache_store,
    request_units, prefix_block_count,
):
    bf16, f32 = jnp.bfloat16, jnp.float32
    vmem = pl.BlockSpec(memory_space=pltpu.VMEM)
    smem = pl.BlockSpec(memory_space=pltpu.SMEM)
    anywhere = pl.BlockSpec(memory_space=pl.ANY)
    shapes = (
        jax.ShapeDtypeStruct((256, 512), bf16),
        jax.ShapeDtypeStruct((256, 1024), bf16),
        jax.ShapeDtypeStruct((2, 16, 64, 256), bf16),
    )
    results = pl.pallas_call(
        kernel,
        out_shape=tuple(pltpu.VMEM(s.shape, s.dtype) for s in shapes),
        in_specs=[smem] * 3 + [vmem] * 3 + [anywhere] * 8,
        out_specs=[vmem] * 3,
        scratch_shapes=[
            pltpu.VMEM((256, 512), bf16),
            pltpu.VMEM((256, 128), bf16),
            pltpu.VMEM((256, 128), bf16),
            pltpu.VMEM((256, 1024), bf16),
            pltpu.VMEM((256, 1024), bf16),
            pltpu.VMEM((256, 256), bf16),
            pltpu.VMEM((256, 256), bf16),
            pltpu.VMEM((UNITS, 2, 128, 128), bf16),
            pltpu.VMEM((24, 128), jnp.int32),
            pltpu.SMEM((24, 128), jnp.int32),
            pltpu.VMEM((7, UNITS, 128, 128), bf16),
            pltpu.VMEM((7, UNITS, 128, 128), bf16),
            pltpu.VMEM((UNITS, 128, 128), bf16),
            pltpu.VMEM((7, 16, 128, 128), bf16),
            pltpu.VMEM((7, 16, 128, 128), bf16),
            pltpu.VMEM((128, 128, 128), bf16),
            pltpu.VMEM((128, 128, 128), bf16),
            pltpu.VMEM((2 * GROUPS, ROWS, GROUP * 128), bf16),
            pltpu.VMEM((2, ROWS, 128), bf16),
            pltpu.VMEM((ROWS, GROUP * 128), f32),
            pltpu.VMEM((2, ROWS, 128), bf16),
            pltpu.VMEM((2, ROWS, 128), f32),
            pltpu.VMEM((2, ROWS, 128), f32),
            pltpu.VMEM((2 * (GROUPS + 1), ROWS, 128), f32),
            pltpu.VMEM((2, ROWS, 128), f32),
            pltpu.VMEM((2, 128, 128), f32),
            pltpu.VMEM((2, 128, 16), f32),
            pltpu.VMEM((2, 128, 16), f32),
            pltpu.VMEM((2, 16, 128), f32),
            pltpu.VMEM((2, 16, 128), f32),
            pltpu.VMEM((256, 1024), f32),
            pltpu.VMEM((256, 1024), f32),
            pltpu.VMEM((256, 1024), f32),
            pltpu.VMEM((16, 128, 256), f32),
            pltpu.VMEM((4, 128, 128), f32),
            pltpu.VMEM((2, 8, 128), f32),
            pltpu.VMEM((7, 2, 8, 128), f32),
            pltpu.SemaphoreType.DMA((28,)),
            pltpu.SemaphoreType.DMA((28,)),
            pltpu.SemaphoreType.DMA((112,)),
            pltpu.SemaphoreType.DMA((112,)),
            pltpu.SemaphoreType.DMA((7,)),
            pltpu.SemaphoreType.DMA((7,)),
            pltpu.SemaphoreType.DMA((8,)),
            pltpu.SemaphoreType.DMA,
        ],
        compiler_params=pltpu.CompilerParams(
            collective_id=0, has_side_effects=True, vmem_limit_bytes=56 << 20
        ),
    )(
        prefix_block_count, decay_log, skip_gain, request_units.T, step_lengths.T,
        gated_norm_gain[None], queries, suffix_key_rows, suffix_value_rows, mamba_input, mamba_gate,
        input_projection, output_projection, cache_store.reshape(UNITS, 2, 128, 128),
    )
    return pl.pallas_call(
        hand_over,
        out_shape=shapes,
        in_specs=[vmem] * 3,
        out_specs=[anywhere] * 3,
        scratch_shapes=[pltpu.SemaphoreType.DMA((3,))],
    )(*(pltpu.with_memory_space_constraint(r, pltpu.VMEM) for r in results))


def solution(mesh):
    placed = (
        P("rep", "tp"),
        P("rep", "tp"),
        P("rep", "tp"),
        P("rep", "tp"),
        P("rep", "tp"),
        P("rep", None),
        P("rep", None),
        P("rep", "tp"),
        P("tp"),
        P("tp"),
        P("tp"),
        P("rep", "tp", None, None, None),
        P(),
        P(),
    )
    return jax.shard_map(
        body,
        mesh=mesh,
        in_specs=placed,
        out_specs=(P("rep", "tp"), P("rep", "tp"), P("rep", "tp", None, None)),
        check_vma=False,
    )
```
